256 devices in a mesh: ctx: 64 (over z, y, core), tp: 4 (over x).
Axes of the slice: x: 4, y: 4, z: 8, core: 2. Of those that a mesh axis runs over, the one named last changes fastest.
Arguments:
- tokens: bfloat16 [65536, 4096], P('ctx', 'tp'), may hold values from -6 to 6
- chosen: int32 [4096], P('ctx'), may hold values from 0 to 65535, as said below
- router: bfloat16 [4096], replicated, may hold values from -0.09375 to 0.09375
- w_query: bfloat16 [4096, 2048], P(None, 'tp')
- w_key: bfloat16 [4096, 512], P(None, 'tp')
- w_value: bfloat16 [4096, 512], P(None, 'tp'), may hold values from -0.09375 to 0.09375
- w_out: bfloat16 [2048, 4096], P('tp'), may hold values from -0.5 to 0.5
- cotangent: bfloat16 [65536, 4096], P('ctx', 'tp'), may hold values from -6 to 6
Outputs:
- mixed: bfloat16 [65536, 4096], P('ctx', 'tp')
- input_grad: bfloat16 [65536, 4096], P('ctx', 'tp')
The draws below stay inside these ranges and needn't reach their ends.
Inputs may be any that keep to these rules, and one draw needn't show every extreme that they name: Entries 64 * b to 64 * (b + 1) - 1 hold, in increasing order, 64 different positions of block b, which is positions 1024 * b to 1024 * (b + 1) - 1. The first and the last position of the sequence are always chosen.
All inputs are finite; a program needn't handle non-finite values.
Results may differ from the reference program's by a relative error of at most 0.011.
Values may be sent and summed in bfloat16 or wider, within the bound.
No kernel may reach another device: no remote copies, remote signals or barrier semaphores. Data moves between devices by JAX's collectives and lax.ppermute only.
A program may use at most 128 MiB of HBM per device.

```python
import math
import jax
import jax.numpy as jnp
from jax import lax

D = 4096
HEADS = 16
KV_HEADS = 4
HEAD_DIM = 128
TOK_DEV = 1024
SEL = 64
TOKENS = 65536
N_CTX = 64


def draw_chosen(key, part):
    key = jax.random.fold_in(key, 11)
    block_keys = jax.random.split(key, N_CTX)

    def one_block(block_key):
        shuffled = jax.random.permutation(block_key, TOK_DEV)
        return jnp.sort(shuffled[:SEL])
    picked = jax.vmap(one_block)(block_keys).astype(jnp.int32)
    picked = picked.at[0, 0].set(0)
    picked = picked.at[N_CTX - 1, SEL - 1].set(TOK_DEV - 1)
    starts = jnp.arange(N_CTX, dtype=jnp.int32)[:, None] * TOK_DEV
    return (picked + starts).reshape(-1)


def draw_w_query(key, part):
    key = jax.random.fold_in(key, 31)
    drawn_part = jax.random.normal(key, (D, HEADS * HEAD_DIM), jnp.float32) / math.sqrt(D)
    return drawn_part.astype(jnp.bfloat16)


def draw_w_key(key, part):
    key = jax.random.fold_in(key, 47)
    drawn_part = jax.random.normal(key, (D, KV_HEADS * HEAD_DIM), jnp.float32) / math.sqrt(D)
    return drawn_part.astype(jnp.bfloat16)


def steps_of(own_key, shape, cuts, least, top_value):
    gain, own = 1.0, jax.random.fold_in(own_key, 6)
    for axis_at, shards_of in cuts:
        heights = jnp.exp(jax.random.uniform(jax.random.fold_in(own, axis_at), (shards_of,), jnp.float32, least / len(cuts), top_value / len(cuts)))
        gain = gain * jnp.repeat(heights, shape[axis_at] // shards_of).reshape([-1 if axis == axis_at else 1 for axis in range(len(shape))])
    return gain


def noise(rng, shape, spread, reach, cuts=(), kind=jnp.bfloat16):
    factor_of = steps_of(rng, shape, cuts, -0.22, 0.18) if cuts else 1.0
    entries = jax.random.normal(rng, shape, jnp.float32) * spread * factor_of
    return jnp.minimum(jnp.maximum(entries, -reach), reach).astype(kind)


def setup_inputs(seed: int = 0) -> dict:
    arg_keys = jax.random.split(jax.random.key(seed), 9)
    tokens = noise(arg_keys[0], (TOKENS, D), 1.0, 6.0, ((0, 64), (1, 4)))
    chosen = draw_chosen(jax.random.fold_in(arg_keys[8], 71), 0)
    router = noise(arg_keys[2], (D,), D ** -0.5, 0.09375)
    w_query = draw_w_query(jax.random.fold_in(arg_keys[8], 71), 0)
    w_key = draw_w_key(jax.random.fold_in(arg_keys[8], 71), 0)
    w_value = noise(arg_keys[5], (D, KV_HEADS * HEAD_DIM), D ** -0.5, 0.09375, ((1, 4),))
    w_out = noise(arg_keys[6], (HEADS * HEAD_DIM, D), HEAD_DIM ** -0.5, 0.5, ((0, 4),))
    cotangent = noise(arg_keys[7], (TOKENS, D), 1.0, 6.0, ((0, 64), (1, 4)))
    return {"tokens": tokens, "chosen": chosen, "router": router, "w_query": w_query, "w_key": w_key, "w_value": w_value, "w_out": w_out, "cotangent": cotangent}


EPS = 1e-05

def head_probs(queries, keys, head_index, allowed):
    group_size = HEADS // KV_HEADS
    query_head = lax.dynamic_slice_in_dim(queries, (head_index * HEAD_DIM).astype(jnp.int32), HEAD_DIM, 1)
    key_start = (head_index // group_size * HEAD_DIM).astype(jnp.int32)
    key_head = lax.dynamic_slice_in_dim(keys, key_start, HEAD_DIM, 1)
    logit_rows = jnp.dot(query_head, key_head.T, preferred_element_type=jnp.float32) * (1.0 / math.sqrt(HEAD_DIM))
    masked_logits = jnp.where(allowed, logit_rows, -jnp.inf)
    row_top = lax.optimization_barrier(jnp.max(masked_logits, axis=1, keepdims=True))
    weights = jnp.exp(masked_logits - row_top)
    probabilities = weights / lax.optimization_barrier(jnp.sum(weights, axis=1, keepdims=True))
    return (probabilities, query_head, key_head, key_start)

def reference(tokens, chosen, router, w_query, w_key, w_value, w_out, cotangent):
    picked_rows = tokens[chosen]
    picked_grad = cotangent[chosen]
    rows_wide = picked_rows.astype(jnp.float32)
    gating = jax.nn.sigmoid(jnp.dot(picked_rows, router, preferred_element_type=jnp.float32))
    inverse = lax.rsqrt(lax.optimization_barrier(jnp.mean(rows_wide * rows_wide, axis=1)) + EPS)
    normed = (rows_wide * inverse[:, None]).astype(jnp.bfloat16)
    queries = jnp.dot(normed, w_query, preferred_element_type=jnp.float32).astype(jnp.bfloat16)
    keys = jnp.dot(normed, w_key, preferred_element_type=jnp.float32).astype(jnp.bfloat16)
    values = jnp.dot(normed, w_value, preferred_element_type=jnp.float32).astype(jnp.bfloat16)
    chosen_total = chosen.shape[0]
    row_ranks = jnp.arange(chosen_total, dtype=jnp.int32)
    allowed = row_ranks[None, :] <= row_ranks[:, None]
    logit_scale = 1.0 / math.sqrt(HEAD_DIM)
    head_list = jnp.arange(HEADS, dtype=jnp.int32)

    def forward_head(head_index):
        probabilities, query_head, key_head, key_start = head_probs(queries, keys, head_index, allowed)
        value_head = lax.dynamic_slice_in_dim(values, key_start, HEAD_DIM, 1)
        return jnp.dot(probabilities.astype(jnp.bfloat16), value_head, preferred_element_type=jnp.float32)
    attended_all = lax.map(forward_head, head_list)
    attended = jnp.transpose(attended_all, (1, 0, 2)).reshape(chosen_total, HEADS * HEAD_DIM).astype(jnp.bfloat16)
    branch = jnp.dot(attended, w_out, preferred_element_type=jnp.float32)
    mixed = tokens.at[chosen].set((rows_wide + gating[:, None] * branch).astype(jnp.bfloat16))
    grad_wide = picked_grad.astype(jnp.float32)
    gate_dot = lax.optimization_barrier(jnp.sum(grad_wide * branch, axis=1))
    logit_grad = gate_dot * gating * (1.0 - gating)
    branch_grad = (gating[:, None] * grad_wide).astype(jnp.bfloat16)
    attended_grad = jnp.dot(branch_grad, w_out.T, preferred_element_type=jnp.float32).astype(jnp.bfloat16)

    def backward_head(head_index):
        probabilities, query_head, key_head, key_start = head_probs(queries, keys, head_index, allowed)
        value_head = lax.dynamic_slice_in_dim(values, key_start, HEAD_DIM, 1)
        grad_head = lax.dynamic_slice_in_dim(attended_grad, (head_index * HEAD_DIM).astype(jnp.int32), HEAD_DIM, 1)
        prob_grad = jnp.dot(grad_head, value_head.T, preferred_element_type=jnp.float32)
        score_grad = probabilities * (prob_grad - lax.optimization_barrier(jnp.sum(probabilities * prob_grad, axis=1, keepdims=True)))
        score_low = score_grad.astype(jnp.bfloat16)
        probs_low = probabilities.astype(jnp.bfloat16)
        query_part = jnp.dot(score_low, key_head, preferred_element_type=jnp.float32) * logit_scale
        key_part = jnp.dot(score_low.T, query_head, preferred_element_type=jnp.float32) * logit_scale
        value_part = jnp.dot(probs_low.T, grad_head, preferred_element_type=jnp.float32)
        return (query_part, key_part, value_part)
    query_parts, key_parts, value_parts = lax.map(backward_head, head_list)
    group_size = HEADS // KV_HEADS
    query_grad = jnp.transpose(query_parts, (1, 0, 2)).reshape(chosen_total, HEADS * HEAD_DIM).astype(jnp.bfloat16)
    key_sum = lax.optimization_barrier(jnp.sum(key_parts.reshape(KV_HEADS, group_size, chosen_total, HEAD_DIM), axis=1))
    value_sum = lax.optimization_barrier(jnp.sum(value_parts.reshape(KV_HEADS, group_size, chosen_total, HEAD_DIM), axis=1))
    key_grad = jnp.transpose(key_sum, (1, 0, 2)).reshape(chosen_total, KV_HEADS * HEAD_DIM).astype(jnp.bfloat16)
    value_grad = jnp.transpose(value_sum, (1, 0, 2)).reshape(chosen_total, KV_HEADS * HEAD_DIM).astype(jnp.bfloat16)
    hidden_grad = jnp.dot(query_grad, w_query.T, preferred_element_type=jnp.float32)
    hidden_grad = hidden_grad + jnp.dot(key_grad, w_key.T, preferred_element_type=jnp.float32)
    hidden_grad = hidden_grad + jnp.dot(value_grad, w_value.T, preferred_element_type=jnp.float32)
    row_stat = lax.optimization_barrier(jnp.mean(hidden_grad * rows_wide, axis=1))
    rows_delta = inverse[:, None] * hidden_grad - rows_wide * (inverse ** 3)[:, None] * row_stat[:, None]
    rows_delta = rows_delta + logit_grad[:, None] * router.astype(jnp.float32)[None, :]
    input_grad = cotangent.at[chosen].set((grad_wide + rows_delta).astype(jnp.bfloat16))
    return (mixed, input_grad)
```

```python
import math

import jax
import jax.numpy as jnp
from jax import lax
from jax.experimental import pallas as pl
from jax.experimental.pallas import tpu as pltpu
from jax.sharding import Mesh
from jax.sharding import PartitionSpec as P

HEAD_DIM = 128
EPS = 1e-05
FLOOR = -1e30
LOG2E = 1.0 / math.log(2.0)
BF = jnp.bfloat16
F32 = jnp.float32
VMEM = pltpu.VMEM
NT = (((1,), (1,)), ((), ()))
NN = (((1,), (0,)), ((), ()))


def mm(left, right, dims):
    return lax.dot_general(left, right, dims, preferred_element_type=F32)


def whole():
    return pl.BlockSpec(memory_space=VMEM)


def pick_rows(array, positions):
    picked, (total, width) = positions.shape[0], array.shape
    block = min(256, total)
    steps = total // block

    def kernel(pos_ref, block_ref, out_ref, acc_ref):
        step = pl.program_id(0)
        column = lax.broadcasted_iota(jnp.int32, (picked, block), 1) + step * block
        chosen_here = jnp.where(column == pos_ref[...], 1.0, 0.0).astype(BF)
        part = mm(chosen_here, block_ref[...], NN)

        @pl.when(step == 0)
        def _():
            acc_ref[...] = part

        @pl.when(step > 0)
        def _():
            acc_ref[...] += part

        @pl.when(step == steps - 1)
        def _():
            out_ref[...] = acc_ref[...].astype(BF)

    return pl.pallas_call(
        kernel,
        grid=(steps,),
        in_specs=[
            pl.BlockSpec((picked, 1), lambda i: (0, 0)),
            pl.BlockSpec((block, width), lambda i: (i, 0)),
        ],
        out_specs=pl.BlockSpec((picked, width), lambda i: (0, 0)),
        out_shape=jax.ShapeDtypeStruct((picked, width), BF),
        scratch_shapes=[pltpu.VMEM((picked, width), F32)],
        name="pick_rows",
    )(positions[:, None], array)


def put_rows(array, positions, rows):
    picked, (total, width) = positions.shape[0], array.shape
    block = min(256, total)

    def kernel(pos_ref, rows_ref, block_ref, out_ref):
        row = lax.broadcasted_iota(jnp.int32, (block, picked), 0) + pl.program_id(0) * block
        here = jnp.where(row == pos_ref[...], 1.0, 0.0)
        value = mm(here.astype(BF), rows_ref[...], NN)
        hit = jnp.max(here, axis=1, keepdims=True) > 0.5
        out_ref[...] = jnp.where(hit, value, block_ref[...].astype(F32)).astype(BF)

    return pl.pallas_call(
        kernel,
        grid=(total // block,),
        in_specs=[
            pl.BlockSpec((1, picked), lambda i: (0, 0)),
            pl.BlockSpec((picked, width), lambda i: (0, 0)),
            pl.BlockSpec((block, width), lambda i: (i, 0)),
        ],
        out_specs=pl.BlockSpec((block, width), lambda i: (i, 0)),
        out_shape=jax.ShapeDtypeStruct((total, width), BF),
        name="put_rows",
    )(positions[None, :], rows, array)


class Tiles:
    def __init__(self, picked, planes, columns, cores, heads):
        self.picked, self.planes, self.columns, self.cores, self.heads = (
            picked, planes, columns, cores, heads,
        )
        self.group = cores * picked
        self.lanes = heads * self.group
        self.keys = planes * picked
        self.half = heads * HEAD_DIM

    def fill(self, place, own, other, group_ref):
        core = place[2]
        mine = pl.ds(pl.multiple_of(core * self.picked, self.picked), self.picked)
        theirs = pl.ds(pl.multiple_of((1 - core) * self.picked, self.picked), self.picked)
        for s in range(self.columns):
            group_ref[s, mine, :] = own[s][...]
            group_ref[s, theirs, :] = other[s][...]

    def stacked(self, group_ref, s, first):
        parts = [
            group_ref[s, :, first + h * HEAD_DIM : first + (h + 1) * HEAD_DIM]
            for h in range(self.heads)
        ]
        return jnp.concatenate(parts, axis=0)

    def y_of(self, place, s):
        return lax.rem(place[1] + self.columns - s, self.columns)

    def scores(self, place, keys, queries, s):
        z, y, core = place[0], place[1], place[2]
        plane_rows = self.columns * self.group
        logits = mm(keys, queries, NT) * (LOG2E / math.sqrt(HEAD_DIM))
        key = lax.broadcasted_iota(jnp.int32, (self.keys, 1), 0)
        key_rank = (
            lax.div(key, self.picked) * plane_rows
            + (y * self.cores + core) * self.picked
            + lax.rem(key, self.picked)
        )
        lane = lax.broadcasted_iota(jnp.int32, (1, self.lanes), 1)
        query_rank = z * plane_rows + self.y_of(place, s) * self.group + lax.rem(lane, self.group)
        return jnp.where(key_rank <= query_rank, logits, FLOOR)


def softmax_parts(tiles, place, own, other, key_values):
    n = tiles.columns

    def kernel(place_ref, kv_ref, *refs):
        own_refs, other_refs, out_ref, group_ref = refs[:n], refs[n : 2 * n], refs[2 * n], refs[-1]
        at = (place_ref[0], place_ref[1], place_ref[2])
        tiles.fill(at, own_refs, other_refs, group_ref)
        keys, values = kv_ref[:, :HEAD_DIM], kv_ref[:, HEAD_DIM:]
        for s in range(n):
            queries = tiles.stacked(group_ref, s, 0)
            grads = tiles.stacked(group_ref, s, tiles.half)
            logits = tiles.scores(at, keys, queries, s)
            top = jnp.max(logits, axis=0, keepdims=True)
            weights = jnp.exp2(logits - top)
            prob_grad = mm(values, grads, NT)
            total = jnp.sum(weights, axis=0, keepdims=True)
            inner = jnp.sum(weights * prob_grad, axis=0, keepdims=True)
            some = top > 0.5 * FLOOR
            slot = tiles.y_of(at, s)
            out_ref[slot, 0:1, :] = top
            out_ref[slot, 1:2, :] = jnp.where(some, total, 0.0)
            out_ref[slot, 2:3, :] = jnp.where(some, inner, 0.0)
            out_ref[slot, 3:4, :] = jnp.zeros_like(top)

    return pl.pallas_call(
        kernel,
        in_specs=[pl.BlockSpec(memory_space=pltpu.SMEM)] + [whole()] * (1 + 2 * n),
        out_specs=whole(),
        out_shape=jax.ShapeDtypeStruct((n, 4, tiles.lanes), F32),
        scratch_shapes=[pltpu.VMEM((n, tiles.group, 2 * tiles.half), BF)],
        compiler_params=pltpu.CompilerParams(vmem_limit_bytes=24 * 2**20),
        name="softmax_parts",
    )(place, key_values, *own, *other)


def attention_parts(tiles, place, own, other, key_values, parts):
    n = tiles.columns
    scale = 1.0 / math.sqrt(HEAD_DIM)

    def kernel(place_ref, kv_ref, parts_ref, *refs):
        own_refs, other_refs = refs[:n], refs[n : 2 * n]
        mine_ref, theirs_ref, kv_grad_ref, group_ref, result_ref = refs[2 * n :]
        at = (place_ref[0], place_ref[1], place_ref[2])
        tiles.fill(at, own_refs, other_refs, group_ref)
        keys, values = kv_ref[:, :HEAD_DIM], kv_ref[:, HEAD_DIM:]
        keys_t, values_t = keys.T, values.T
        key_grad = jnp.zeros((tiles.keys, HEAD_DIM), F32)
        value_grad = jnp.zeros((tiles.keys, HEAD_DIM), F32)
        core = at[2]
        mine = pl.ds(pl.multiple_of(core * tiles.picked, tiles.picked), tiles.picked)
        theirs = pl.ds(pl.multiple_of((1 - core) * tiles.picked, tiles.picked), tiles.picked)
        for s in range(n):
            slot = tiles.y_of(at, s)
            tops = [parts_ref[b, slot, 0:1, :] for b in range(n * tiles.cores)]
            top = tops[0]
            for one in tops[1:]:
                top = jnp.maximum(top, one)
            total, inner = jnp.zeros_like(top), jnp.zeros_like(top)
            for b in range(n * tiles.cores):
                weight = jnp.exp2(tops[b] - top)
                total += weight * parts_ref[b, slot, 1:2, :]
                inner += weight * parts_ref[b, slot, 2:3, :]
            shift = top + jnp.log(total) * LOG2E
            row_inner = inner / total
            queries = tiles.stacked(group_ref, s, 0)
            grads = tiles.stacked(group_ref, s, tiles.half)
            probs = jnp.exp2(tiles.scores(at, keys, queries, s) - shift)
            prob_grad = mm(values, grads, NT)
            score_low = (probs * (prob_grad - row_inner)).astype(BF)
            probs_low = probs.astype(BF)
            key_grad += mm(score_low, queries, NN)
            value_grad += mm(probs_low, grads, NN)
            query_t = mm(keys_t, score_low, NN) * scale
            output_t = mm(values_t, probs_low, NN)
            for h in range(tiles.heads):
                lanes = slice(h * tiles.group, (h + 1) * tiles.group)
                columns = slice(h * HEAD_DIM, (h + 1) * HEAD_DIM)
                shifted = slice(tiles.half + h * HEAD_DIM, tiles.half + (h + 1) * HEAD_DIM)
                result_ref[s, :, columns] = query_t[:, lanes].T.astype(BF)
                result_ref[s, :, shifted] = output_t[:, lanes].T.astype(BF)
            mine_ref[s, :, :] = result_ref[s, mine, :]
            theirs_ref[s, :, :] = result_ref[s, theirs, :]
        kv_grad_ref[:, :HEAD_DIM] = (key_grad * scale).astype(BF)
        kv_grad_ref[:, HEAD_DIM:] = value_grad.astype(BF)

    rows = jax.ShapeDtypeStruct((n, tiles.picked, 2 * tiles.half), BF)
    return pl.pallas_call(
        kernel,
        in_specs=[pl.BlockSpec(memory_space=pltpu.SMEM)] + [whole()] * (2 + 2 * n),
        out_specs=[whole()] * 3,
        out_shape=[rows, rows, jax.ShapeDtypeStruct((tiles.keys, 2 * HEAD_DIM), BF)],
        scratch_shapes=[pltpu.VMEM((n, tiles.group, 2 * tiles.half), BF)] * 2,
        compiler_params=pltpu.CompilerParams(vmem_limit_bytes=24 * 2**20),
        name="attention_parts",
    )(place, key_values, parts, *own, *other)


def copies(array, count):
    return jnp.broadcast_to(array[None], (count,) + array.shape)


def exchange(array, axis):
    return lax.all_to_all(array, axis, 0, 0, tiled=True)


def shifted(array, axis, count, step):
    return lax.ppermute(array, axis, [(i, (i + step) % count) for i in range(count)])


def on_device(sizes, tokens, chosen, router, w_query, w_key, w_value, w_out, cotangent):
    planes, columns, cores, parts_tp = sizes
    picked = chosen.shape[0]
    tok_rows, part_width = tokens.shape
    width = part_width * parts_tp
    z, y, core, tp = (lax.axis_index(name) for name in ("z", "y", "core", "tp"))
    local_rows = chosen - ((z * columns + y) * cores + core) * tok_rows
    heads = w_query.shape[1] // HEAD_DIM
    tiles = Tiles(picked, planes, columns, cores, heads)
    half = tiles.half

    rows_in = pick_rows(tokens, local_rows)
    rows_grad = pick_rows(cotangent, local_rows)
    in_parts = exchange(copies(rows_in, parts_tp), "tp")
    full_in = jnp.transpose(in_parts, (1, 0, 2)).reshape(picked, width)
    full_grad = jnp.zeros((picked, width), BF)
    for s in range(parts_tp):
        piece = rows_grad if s == 0 else shifted(rows_grad, "tp", parts_tp, s)
        owner = lax.rem(tp + parts_tp - s, parts_tp)
        full_grad = lax.dynamic_update_slice(full_grad, piece, (0, owner * part_width))

    wide_in = full_in.astype(F32)
    inverse = lax.rsqrt(jnp.mean(wide_in * wide_in, axis=1) + EPS)
    gating = jax.nn.sigmoid(jnp.dot(full_in, router, preferred_element_type=F32))
    normed = (wide_in * inverse[:, None]).astype(BF)
    keys_own = mm(normed, w_key, NN).astype(BF)
    values_own = mm(normed, w_value, NN).astype(BF)
    key_values = exchange(copies(jnp.concatenate([keys_own, values_own], axis=1), planes), "z")
    key_values = key_values.reshape(planes * picked, 2 * HEAD_DIM)
    queries = mm(normed, w_query, NN).astype(BF)
    branch_grad = (gating[:, None] * full_grad.astype(F32)).astype(BF)
    attended_grad = mm(branch_grad, w_out, NT).astype(BF)

    own = [jnp.concatenate([queries, attended_grad], axis=1)]
    own = own + [shifted(own[0], "y", columns, s) for s in range(1, columns)]
    other = [shifted(piece, "core", cores, 1) for piece in own]
    place = jnp.stack([z, y, core]).astype(jnp.int32)
    parts = softmax_parts(tiles, place, own, other, key_values)
    parts = exchange(copies(parts, columns * cores), ("y", "core"))
    mine, theirs, kv_grads = attention_parts(tiles, place, own, other, key_values, parts)

    kv_grads = exchange(kv_grads.reshape(planes, picked, 2 * HEAD_DIM), "z")
    received = shifted(theirs, "core", cores, 1)
    chip = (mine.astype(F32) + received.astype(F32)).astype(BF)
    total = chip[0].astype(F32)
    for s in range(1, columns):
        total = total + shifted(chip[s], "y", columns, columns - s).astype(F32)
    total = total.astype(BF)
    query_grad, attended = total[:, :half], total[:, half:]
    kv_grad = jnp.sum(kv_grads.astype(F32), axis=0).astype(BF)

    branch_part = mm(attended, w_out, NN)
    hidden_part = mm(query_grad, w_query, NT)
    hidden_part = hidden_part + mm(kv_grad[:, :HEAD_DIM], w_key, NT)
    hidden_part = hidden_part + mm(kv_grad[:, HEAD_DIM:], w_value, NT)
    stat_part = jnp.sum(hidden_part * wide_in, axis=1) * (1.0 / width)
    gate_part = jnp.sum(attended.astype(F32) * attended_grad.astype(F32), axis=1)
    scalars = jnp.stack([stat_part, gate_part], axis=1)
    high = scalars.astype(BF)
    low = (scalars - high.astype(F32)).astype(BF)
    extra = jnp.concatenate([high, low, jnp.zeros((picked, 124), BF)], axis=1)

    def by_owner(array):
        pieces = array.astype(BF).reshape(picked, parts_tp, part_width)
        return jnp.transpose(pieces, (1, 0, 2))

    sent = jnp.concatenate(
        [by_owner(hidden_part), by_owner(branch_part), copies(extra, parts_tp)], axis=2
    )
    summed = jnp.sum(exchange(sent, "tp").astype(F32), axis=0)
    hidden = summed[:, :part_width]
    branch = summed[:, part_width : 2 * part_width]
    row_stat = summed[:, 2 * part_width] + summed[:, 2 * part_width + 2]
    gate_sum = summed[:, 2 * part_width + 1] + summed[:, 2 * part_width + 3]

    wide_own = rows_in.astype(F32)
    mixed_rows = (wide_own + gating[:, None] * branch).astype(BF)
    mixed = put_rows(tokens, local_rows, mixed_rows)
    logit_grad = gate_sum * (1.0 - gating)
    router_own = lax.dynamic_slice_in_dim(router, tp * part_width, part_width, 0).astype(F32)
    delta = inverse[:, None] * hidden - wide_own * (inverse**3 * row_stat)[:, None]
    delta = delta + logit_grad[:, None] * router_own[None, :]
    grad_rows = (rows_grad.astype(F32) + delta).astype(BF)
    input_grad = put_rows(cotangent, local_rows, grad_rows)
    return mixed, input_grad


def solution(mesh):
    sizes = (8, 4, 2, 4)
    return build(mesh, sizes)


def build(mesh, sizes):
    fine = Mesh(mesh.devices.reshape(sizes), ("z", "y", "core", "tp"))
    ctx = ("z", "y", "core")

    def step(*arrays):
        return on_device(sizes, *arrays)

    placed = (
        P(ctx, "tp"), P(ctx), P(), P(None, "tp"), P(None, "tp"), P(None, "tp"), P("tp", None), P(ctx, "tp"),
    )
    return jax.shard_map(
        step,
        mesh=fine,
        in_specs=placed,
        out_specs=(P(ctx, "tp"), P(ctx, "tp")),
        check_vma=False,
    )
```

```python
import math

import jax
import jax.numpy as jnp
from jax import lax
from jax.experimental import pallas as pl
from jax.experimental.pallas import tpu as pltpu
from jax.sharding import Mesh
from jax.sharding import PartitionSpec as P

HEAD_DIM = 128
EPS = 1e-05
FLOOR = -1e30
LOG2E = 1.0 / math.log(2.0)
BF = jnp.bfloat16
F32 = jnp.float32
VMEM = pltpu.VMEM
NT = (((1,), (1,)), ((), ()))
NN = (((1,), (0,)), ((), ()))


def mm(left, right, dims):
    return lax.dot_general(left, right, dims, preferred_element_type=F32)


def whole():
    return pl.BlockSpec(memory_space=VMEM)


def far():
    return pl.BlockSpec(memory_space=pl.ANY)


def like(shape, dtype=BF):
    return jax.ShapeDtypeStruct(tuple(shape), dtype)


def params(mib):
    return pltpu.CompilerParams(vmem_limit_bytes=mib * 2**20)


def my_place():
    return lax.axis_index("z"), lax.axis_index("y"), lax.axis_index("core")


def my_first_row(sizes, tok_rows):
    z, y, core = my_place()
    return ((z * sizes[1] + y) * sizes[2] + core) * tok_rows


def pick_rows(sizes, array, chosen):
    picked = chosen.shape[1]
    total, width = array.shape
    rows = min(256, total)

    def kernel(chosen_ref, array_ref, out_ref):
        square = (picked, picked)
        eye = lax.broadcasted_iota(jnp.int32, square, 0) == lax.broadcasted_iota(jnp.int32, square, 1)
        local = (chosen_ref[...] - my_first_row(sizes, total)).astype(F32)
        spot = jnp.sum(jnp.where(eye, jnp.broadcast_to(local, square), 0.0), axis=1, keepdims=True)
        column = lax.broadcasted_iota(jnp.int32, (picked, total), 1)
        here = jnp.where(column == spot.astype(jnp.int32), 1.0, 0.0).astype(BF)
        out_ref[...] = mm(here, array_ref[...], NN).astype(BF)

    return pl.pallas_call(
        kernel,
        in_specs=[whole()] * 2,
        out_specs=whole(),
        out_shape=like((picked, width)),
        compiler_params=params(8),
        name="pick_rows",
    )(chosen, array)


def project(sizes, in_pieces, grad_pieces, router, w_query, w_key, w_value, w_out, after):
    parts = len(in_pieces)
    picked, part = in_pieces[0].shape
    width = part * parts
    half = w_query.shape[1]

    def kernel(*refs):
        in_refs, grad_refs = refs[:parts], refs[parts : 2 * parts]
        router_ref, query_ref, key_ref, value_ref, out_w_ref = refs[2 * parts : 2 * parts + 5]
        kv_ref, own_ref, scales_ref = refs[2 * parts + 6 :]
        tp = lax.axis_index("tp")

        def span(s):
            owner = lax.rem(tp + parts - s, parts)
            return pl.ds(pl.multiple_of(owner * part, part), part)

        squares = jnp.zeros((picked, 1), F32)
        logit = jnp.zeros((picked, 1), F32)
        for s in range(parts):
            rows = in_refs[s][...].astype(F32)
            squares += jnp.sum(rows * rows, axis=1, keepdims=True)
            weights = router_ref[:, span(s)].astype(F32)
            logit += jnp.sum(rows * weights, axis=1, keepdims=True)
        inverse = lax.rsqrt(squares * (1.0 / width) + EPS)
        gate = 1.0 / (1.0 + jnp.exp(-logit))
        lane = lax.broadcasted_iota(jnp.int32, (picked, 128), 1)
        scales_ref[...] = jnp.where(lane == 0, gate, inverse)
        keys = jnp.zeros((picked, HEAD_DIM), F32)
        values = jnp.zeros((picked, HEAD_DIM), F32)
        queries = jnp.zeros((picked, half), F32)
        grads = jnp.zeros((picked, half), F32)
        for s in range(parts):
            rows = span(s)
            normed = (in_refs[s][...].astype(F32) * inverse).astype(BF)
            keys += mm(normed, key_ref[rows, :], NN)
            values += mm(normed, value_ref[rows, :], NN)
            queries += mm(normed, query_ref[rows, :], NN)
            grads += mm(grad_refs[s][...], out_w_ref[:, rows], NT)
        own_ref[:, :half] = queries.astype(BF)
        own_ref[:, half:] = (gate * grads).astype(BF)
        low = jnp.concatenate([keys, values], axis=1).astype(BF)
        for b in range(sizes[0]):
            kv_ref[b] = low

    ins = (*in_pieces, *grad_pieces, router, w_query, w_key, w_value, w_out)
    outs = [
        like((sizes[0], picked, 2 * HEAD_DIM)),
        like((picked, 2 * half)),
        like((picked, 128), F32),
    ]
    return pl.pallas_call(
        kernel,
        in_specs=[whole()] * len(ins) + [far()],
        out_specs=[whole()] * len(outs),
        out_shape=outs,
        compiler_params=params(16),
        name="project",
    )(*ins, after)


def add_pieces(mine, received):
    count = mine.shape[0]

    def kernel(mine_ref, received_ref, *out_refs):
        for s in range(count):
            out_refs[s][...] = (mine_ref[s].astype(F32) + received_ref[s].astype(F32)).astype(BF)

    outs = [like(mine.shape[1:])] * count
    return pl.pallas_call(
        kernel,
        in_specs=[whole()] * 2,
        out_specs=[whole()] * len(outs),
        out_shape=outs,
        compiler_params=params(8),
        name="add_pieces",
    )(mine, received)


def touch(arrays, after):
    def kernel(*refs):
        refs[-1][...] = jnp.zeros_like(refs[-1])

    return pl.pallas_call(
        kernel,
        in_specs=[whole()] * len(arrays) + [far()],
        out_specs=whole(),
        out_shape=like((8, 128), F32),
        compiler_params=params(4),
        name="touch",
    )(*arrays, after)


def final_shares(pieces, kv_grads, in_pieces, own, w_query, w_key, w_value, w_out, after):
    count, parts = len(pieces), len(in_pieces)
    picked, part = in_pieces[0].shape
    half = w_query.shape[1]

    def kernel(*refs):
        piece_refs, in_refs = refs[:count], refs[count : count + parts]
        kv_ref, own_ref, query_ref, key_ref, value_ref, out_w_ref, _ = refs[
            count + parts : count + parts + 7
        ]
        out_refs = refs[count + parts + 7 :]
        tp = lax.axis_index("tp")
        total = piece_refs[0][...].astype(F32)
        for ref in piece_refs[1:]:
            total += ref[...].astype(F32)
        total = total.astype(BF)
        query_grad, attended = total[:, :half], total[:, half:]
        kv_sum = kv_ref[0].astype(F32)
        for b in range(1, kv_ref.shape[0]):
            kv_sum += kv_ref[b].astype(F32)
        kv_sum = kv_sum.astype(BF)
        key_grad, value_grad = kv_sum[:, :HEAD_DIM], kv_sum[:, HEAD_DIM:]
        stat = jnp.zeros((picked, 1), F32)
        for s in range(parts):
            owner = lax.rem(tp + s, parts)
            rows = pl.ds(pl.multiple_of(owner * part, part), part)
            hidden = mm(query_grad, query_ref[rows, :], NT)
            hidden += mm(key_grad, key_ref[rows, :], NT)
            hidden += mm(value_grad, value_ref[rows, :], NT)
            rows_in = in_refs[(parts - s) % parts][...].astype(F32)
            stat += jnp.sum(hidden * rows_in, axis=1, keepdims=True)
            out_refs[s][:, :part] = hidden.astype(BF)
            out_refs[s][:, part : 2 * part] = mm(attended, out_w_ref[:, rows], NN).astype(BF)
        stat = stat * (1.0 / (part * parts))
        grads = own_ref[:, half:].astype(F32)
        gate_sum = jnp.sum(attended.astype(F32) * grads, axis=1, keepdims=True)
        stat_high, gate_high = stat.astype(BF).astype(F32), gate_sum.astype(BF).astype(F32)
        lane = lax.broadcasted_iota(jnp.int32, (picked, 128), 1)
        extra = jnp.where(lane == 0, stat_high, 0.0)
        extra = jnp.where(lane == 1, gate_high, extra)
        extra = jnp.where(lane == 2, stat - stat_high, extra)
        extra = jnp.where(lane == 3, gate_sum - gate_high, extra).astype(BF)
        for s in range(parts):
            out_refs[s][:, 2 * part :] = extra

    ins = (*pieces, *in_pieces, kv_grads, own, w_query, w_key, w_value, w_out)
    outs = [like((picked, 2 * part + 128))] * parts
    return pl.pallas_call(
        kernel,
        in_specs=[whole()] * len(ins) + [far()],
        out_specs=[whole()] * parts,
        out_shape=outs,
        compiler_params=params(16),
        name="final_shares",
    )(*ins, after)


def put_block(base, spot, new, i, rows):
    row = lax.broadcasted_iota(jnp.int32, (rows, spot.shape[1]), 0)
    here = jnp.where(row + i * rows == spot, 1.0, 0.0)
    hit = jnp.max(here, axis=1, keepdims=True) > 0.5
    return jnp.where(hit, mm(here.astype(BF), new, NN), base.astype(F32)).astype(BF)


def put_rows(sizes, tokens, cotangent, chosen, rows_in, rows_grad, shares, scales, router):
    (total, width), parts = cotangent.shape, sizes[3]
    rows = min(128, total)
    steps = total // rows

    def kernel(chosen_ref, in_ref, grad_ref, scales_ref, router_ref, tokens_ref, cotangent_ref, *refs):
        share_refs = refs[:parts]
        mixed_ref, input_grad_ref, block_ref, sems = refs[parts:]
        tp = lax.axis_index("tp")
        gating, inverse_rows = scales_ref[:, 0:1], scales_ref[:, 1:2]
        wide_in = in_ref[...].astype(F32)
        summed = share_refs[0][...].astype(F32)
        for ref in share_refs[1:]:
            summed += ref[...].astype(F32)
        hidden, branch, extra = summed[:, :width], summed[:, width : 2 * width], summed[:, 2 * width :]
        row_stat = extra[:, 0:1] + extra[:, 2:3]
        logit_grad = (extra[:, 1:2] + extra[:, 3:4]) * (1.0 - gating)
        router_own = router_ref[:, pl.ds(pl.multiple_of(tp * width, width), width)].astype(F32)
        delta = inverse_rows * hidden - wide_in * (inverse_rows**3 * row_stat)
        delta = delta + logit_grad * router_own
        grad_rows = (grad_ref[...].astype(F32) + delta).astype(BF)
        mixed_rows = (wide_in + gating * branch).astype(BF)
        spot = chosen_ref[...] - my_first_row(sizes, total)
        started = []
        pairs = ((tokens_ref, mixed_rows, mixed_ref), (cotangent_ref, grad_rows, input_grad_ref))
        for i in range(steps):
            part = slice(i * rows, (i + 1) * rows)
            for a, (base_ref, new, out_ref) in enumerate(pairs):
                block_ref[a, part, :] = put_block(base_ref[part, :], spot, new, i, rows)
                copy = pltpu.make_async_copy(block_ref.at[a, part], out_ref.at[part], sems.at[a, i])
                copy.start()
                started.append(copy)
        for copy in started:
            copy.wait()

    ins = (chosen, rows_in, rows_grad, scales, router, tokens, cotangent, *shares)
    return pl.pallas_call(
        kernel,
        in_specs=[whole()] * len(ins),
        out_specs=[far()] * 2,
        out_shape=[like((total, width))] * 2,
        scratch_shapes=[pltpu.VMEM((2, total, width), BF), pltpu.SemaphoreType.DMA((2, steps))],
        compiler_params=params(16),
        name="put_rows",
    )(*ins)


class Tiles:
    def __init__(self, picked, planes, columns, cores, heads):
        self.picked, self.planes, self.columns, self.cores, self.heads = (
            picked, planes, columns, cores, heads,
        )
        self.group = cores * picked
        self.lanes = heads * self.group
        self.keys = planes * picked
        self.half = heads * HEAD_DIM

    def fill(self, place, own, other, group_ref):
        core = place[2]
        mine = pl.ds(pl.multiple_of(core * self.picked, self.picked), self.picked)
        theirs = pl.ds(pl.multiple_of((1 - core) * self.picked, self.picked), self.picked)
        for s in range(self.columns):
            group_ref[s, mine, :] = own[s][...]
            group_ref[s, theirs, :] = other[s][...]

    def stacked(self, group_ref, s, first):
        parts = [
            group_ref[s, :, first + h * HEAD_DIM : first + (h + 1) * HEAD_DIM]
            for h in range(self.heads)
        ]
        return jnp.concatenate(parts, axis=0)

    def y_of(self, place, s):
        return lax.rem(place[1] + self.columns - s, self.columns)

    def scores(self, place, keys, queries, s):
        z, y, core = place[0], place[1], place[2]
        plane_rows = self.columns * self.group
        logits = mm(keys, queries, NT) * (LOG2E / math.sqrt(HEAD_DIM))
        key = lax.broadcasted_iota(jnp.int32, (self.keys, 1), 0)
        key_rank = (
            lax.div(key, self.picked) * plane_rows
            + (y * self.cores + core) * self.picked
            + lax.rem(key, self.picked)
        )
        lane = lax.broadcasted_iota(jnp.int32, (1, self.lanes), 1)
        query_rank = z * plane_rows + self.y_of(place, s) * self.group + lax.rem(lane, self.group)
        return jnp.where(key_rank <= query_rank, logits, FLOOR)


def softmax_parts(tiles, own, other, key_values):
    n = tiles.columns

    def kernel(kv_ref, *refs):
        own_refs, other_refs, out_ref, group_ref = refs[:n], refs[n : 2 * n], refs[2 * n], refs[-1]
        at = my_place()
        tiles.fill(at, own_refs, other_refs, group_ref)
        keys, values = kv_ref[:, :HEAD_DIM], kv_ref[:, HEAD_DIM:]
        for s in range(n):
            queries = tiles.stacked(group_ref, s, 0)
            grads = tiles.stacked(group_ref, s, tiles.half)
            logits = tiles.scores(at, keys, queries, s)
            top = jnp.max(logits, axis=0, keepdims=True)
            weights = jnp.exp2(logits - top)
            prob_grad = mm(values, grads, NT)
            total = jnp.sum(weights, axis=0, keepdims=True)
            inner = jnp.sum(weights * prob_grad, axis=0, keepdims=True)
            some = top > 0.5 * FLOOR
            slot = tiles.y_of(at, s)
            out_ref[slot, 0:1, :] = jnp.where(some, top + jnp.log(total) * LOG2E, FLOOR)
            out_ref[slot, 1:2, :] = jnp.where(some, inner / total, 0.0)

    return pl.pallas_call(
        kernel,
        in_specs=[whole()] * (1 + 2 * n),
        out_specs=whole(),
        out_shape=jax.ShapeDtypeStruct((n, 2, tiles.lanes), F32),
        scratch_shapes=[pltpu.VMEM((n, tiles.group, 2 * tiles.half), BF)],
        compiler_params=params(24),
        name="softmax_parts",
    )(key_values, *own, *other)


def attention_parts(tiles, own, other, key_values, parts):
    n = tiles.columns
    scale = 1.0 / math.sqrt(HEAD_DIM)

    def kernel(kv_ref, parts_ref, *refs):
        own_refs, other_refs = refs[:n], refs[n : 2 * n]
        mine_ref, theirs_ref, kv_grad_ref, group_ref, result_ref = refs[2 * n :]
        at = my_place()
        tiles.fill(at, own_refs, other_refs, group_ref)
        keys, values = kv_ref[:, :HEAD_DIM], kv_ref[:, HEAD_DIM:]
        keys_t, values_t = keys.T, values.T
        key_grad = jnp.zeros((tiles.keys, HEAD_DIM), F32)
        value_grad = jnp.zeros((tiles.keys, HEAD_DIM), F32)
        core = at[2]
        mine = pl.ds(pl.multiple_of(core * tiles.picked, tiles.picked), tiles.picked)
        theirs = pl.ds(pl.multiple_of((1 - core) * tiles.picked, tiles.picked), tiles.picked)
        for s in range(n):
            slot = tiles.y_of(at, s)
            tops = [parts_ref[b, slot, 0:1, :] for b in range(n * tiles.cores)]
            top = tops[0]
            for one in tops[1:]:
                top = jnp.maximum(top, one)
            total, inner = jnp.zeros_like(top), jnp.zeros_like(top)
            for b in range(n * tiles.cores):
                weight = jnp.exp2(tops[b] - top)
                total += weight
                inner += weight * parts_ref[b, slot, 1:2, :]
            shift = top + jnp.log(total) * LOG2E
            row_inner = inner / total
            queries = tiles.stacked(group_ref, s, 0)
            grads = tiles.stacked(group_ref, s, tiles.half)
            probs = jnp.exp2(tiles.scores(at, keys, queries, s) - shift)
            prob_grad = mm(values, grads, NT)
            score_low = (probs * (prob_grad - row_inner)).astype(BF)
            probs_low = probs.astype(BF)
            key_grad += mm(score_low, queries, NN)
            value_grad += mm(probs_low, grads, NN)
            query_t = mm(keys_t, score_low, NN) * scale
            output_t = mm(values_t, probs_low, NN)
            for h in range(tiles.heads):
                lanes = slice(h * tiles.group, (h + 1) * tiles.group)
                columns = slice(h * HEAD_DIM, (h + 1) * HEAD_DIM)
                shifted = slice(tiles.half + h * HEAD_DIM, tiles.half + (h + 1) * HEAD_DIM)
                result_ref[s, :, columns] = query_t[:, lanes].T.astype(BF)
                result_ref[s, :, shifted] = output_t[:, lanes].T.astype(BF)
            mine_ref[s, :, :] = result_ref[s, mine, :]
            theirs_ref[s, :, :] = result_ref[s, theirs, :]
        kv_grad_ref[:, :HEAD_DIM] = (key_grad * scale).astype(BF)
        kv_grad_ref[:, HEAD_DIM:] = value_grad.astype(BF)

    rows = like((n, tiles.picked, 2 * tiles.half))
    outs = [rows, rows, like((tiles.keys, 2 * HEAD_DIM))]
    return pl.pallas_call(
        kernel,
        in_specs=[whole()] * (2 + 2 * n),
        out_specs=[whole()] * 3,
        out_shape=outs,
        scratch_shapes=[pltpu.VMEM((n, tiles.group, 2 * tiles.half), BF)] * 2,
        compiler_params=params(24),
        name="attention_parts",
    )(key_values, parts, *own, *other)


def copies(array, count):
    return jnp.broadcast_to(array[None], (count,) + array.shape)


def exchange(array, axis):
    return lax.all_to_all(array, axis, 0, 0, tiled=True)


def shifted(array, axis, count, step):
    return lax.ppermute(array, axis, [(i, (i + step) % count) for i in range(count)])


def on_device(sizes, tokens, chosen, router, w_query, w_key, w_value, w_out, cotangent):
    planes, columns, cores, parts_tp = sizes
    picked = chosen.shape[0]
    chosen, router = chosen[None, :], router[None, :]
    tiles = Tiles(picked, planes, columns, cores, w_query.shape[1] // HEAD_DIM)

    rows_in = pick_rows(sizes, tokens, chosen)
    inputs = [rows_in] + [shifted(rows_in, "tp", parts_tp, s) for s in range(1, parts_tp)]
    rows_grad = pick_rows(sizes, cotangent, chosen)
    grads = [rows_grad] + [shifted(rows_grad, "tp", parts_tp, s) for s in range(1, parts_tp)]
    near = touch((w_out, w_key, w_value), rows_in)
    key_values, mine, scales = project(
        sizes, inputs, grads, router, w_query, w_key, w_value, w_out, near
    )
    own = [mine] + [shifted(mine, "y", columns, s) for s in range(1, columns)]
    key_values = exchange(key_values, "z").reshape(tiles.keys, 2 * HEAD_DIM)
    key_values, *own = lax.optimization_barrier((key_values, *own))
    other = [shifted(piece, "core", cores, 1) for piece in own]
    parts = softmax_parts(tiles, own, other, key_values)
    parts = exchange(copies(parts, columns * cores), ("y", "core"))
    mine, theirs, kv_grads = attention_parts(tiles, own, other, key_values, parts)

    kv_grads = exchange(kv_grads.reshape(planes, picked, 2 * HEAD_DIM), "z")
    chip = add_pieces(mine, shifted(theirs, "core", cores, 1))
    pieces = [chip[0]] + [shifted(chip[s], "y", columns, columns - s) for s in range(1, columns)]
    shares = final_shares(
        pieces, kv_grads, inputs, own[0], w_query, w_key, w_value, w_out, kv_grads
    )
    shares = [shares[0]] + [shifted(shares[s], "tp", parts_tp, s) for s in range(1, parts_tp)]
    mixed, input_grad = put_rows(
        sizes, tokens, cotangent, chosen, rows_in, rows_grad, shares, scales, router
    )
    return mixed, input_grad


def solution(mesh):
    sizes = (8, 4, 2, 4)
    return build(mesh, sizes)


def build(mesh, sizes):
    fine = Mesh(mesh.devices.reshape(sizes), ("z", "y", "core", "tp"))
    ctx = ("z", "y", "core")

    def step(*arrays):
        return on_device(sizes, *arrays)

    placed = (
        P(ctx, "tp"), P(ctx), P(), P(None, "tp"), P(None, "tp"), P(None, "tp"), P("tp", None), P(ctx, "tp"),
    )
    return jax.shard_map(
        step,
        mesh=fine,
        in_specs=placed,
        out_specs=(P(ctx, "tp"), P(ctx, "tp")),
        check_vma=False,
    )
```

```python
import math

import jax
import jax.numpy as jnp
from jax import lax
from jax.experimental import pallas as pl
from jax.experimental.pallas import tpu as pltpu
from jax.sharding import Mesh
from jax.sharding import PartitionSpec as P

HEAD_DIM = 128
EPS = 1e-05
FLOOR = -1e30
LOG2E = 1.0 / math.log(2.0)
BF = jnp.bfloat16
F32 = jnp.float32
VMEM = pltpu.VMEM
NT = (((1,), (1,)), ((), ()))
NN = (((1,), (0,)), ((), ()))


def mm(left, right, dims):
    return lax.dot_general(left, right, dims, preferred_element_type=F32)


def whole():
    return pl.BlockSpec(memory_space=VMEM)


def far():
    return pl.BlockSpec(memory_space=pl.ANY)


def like(shape, dtype=BF):
    return jax.ShapeDtypeStruct(tuple(shape), dtype)


def params(mib):
    return pltpu.CompilerParams(vmem_limit_bytes=mib * 2**20)


def my_place():
    return lax.axis_index("z"), lax.axis_index("y"), lax.axis_index("core")


def my_first_row(sizes, tok_rows):
    z, y, core = my_place()
    return ((z * sizes[1] + y) * sizes[2] + core) * tok_rows


def pick_rows(sizes, array, chosen):
    picked = chosen.shape[1]
    total, width = array.shape
    rows = min(256, total)

    def kernel(chosen_ref, array_ref, out_ref):
        square = (picked, picked)
        eye = lax.broadcasted_iota(jnp.int32, square, 0) == lax.broadcasted_iota(jnp.int32, square, 1)
        local = (chosen_ref[...] - my_first_row(sizes, total)).astype(F32)
        spot = jnp.sum(jnp.where(eye, jnp.broadcast_to(local, square), 0.0), axis=1, keepdims=True)
        column = lax.broadcasted_iota(jnp.int32, (picked, total), 1)
        here = jnp.where(column == spot.astype(jnp.int32), 1.0, 0.0).astype(BF)
        out_ref[...] = mm(here, array_ref[...], NN).astype(BF)

    return pl.pallas_call(
        kernel,
        in_specs=[whole()] * 2,
        out_specs=whole(),
        out_shape=like((picked, width)),
        compiler_params=params(8),
        name="pick_rows",
    )(chosen, array)


def project(sizes, in_pieces, grad_pieces, router, w_query, w_key, w_value, w_out, after):
    parts = len(in_pieces)
    picked, part = in_pieces[0].shape
    width = part * parts
    half = w_query.shape[1]

    def kernel(*refs):
        in_refs, grad_refs = refs[:parts], refs[parts : 2 * parts]
        router_ref, query_ref, key_ref, value_ref, out_w_ref = refs[2 * parts : 2 * parts + 5]
        kv_ref, own_ref, scales_ref = refs[2 * parts + 6 :]
        tp = lax.axis_index("tp")

        def span(s):
            owner = lax.rem(tp + parts - s, parts)
            return pl.ds(pl.multiple_of(owner * part, part), part)

        squares = jnp.zeros((picked, 1), F32)
        logit = jnp.zeros((picked, 1), F32)
        for s in range(parts):
            rows = in_refs[s][...].astype(F32)
            squares += jnp.sum(rows * rows, axis=1, keepdims=True)
            weights = router_ref[:, span(s)].astype(F32)
            logit += jnp.sum(rows * weights, axis=1, keepdims=True)
        inverse = lax.rsqrt(squares * (1.0 / width) + EPS)
        gate = 1.0 / (1.0 + jnp.exp(-logit))
        lane = lax.broadcasted_iota(jnp.int32, (picked, 128), 1)
        scales_ref[...] = jnp.where(lane == 0, gate, inverse)
        keys = jnp.zeros((picked, HEAD_DIM), F32)
        values = jnp.zeros((picked, HEAD_DIM), F32)
        queries = jnp.zeros((picked, half), F32)
        grads = jnp.zeros((picked, half), F32)
        for s in range(parts):
            rows = span(s)
            normed = (in_refs[s][...].astype(F32) * inverse).astype(BF)
            keys += mm(normed, key_ref[rows, :], NN)
            values += mm(normed, value_ref[rows, :], NN)
            queries += mm(normed, query_ref[rows, :], NN)
            grads += mm(grad_refs[s][...], out_w_ref[:, rows], NT)
        own_ref[:, :half] = queries.astype(BF)
        own_ref[:, half:] = (gate * grads).astype(BF)
        low = jnp.concatenate([keys, values], axis=1).astype(BF)
        for b in range(sizes[0]):
            kv_ref[b] = low

    ins = (*in_pieces, *grad_pieces, router, w_query, w_key, w_value, w_out)
    outs = [
        like((sizes[0], picked, 2 * HEAD_DIM)),
        like((picked, 2 * half)),
        like((picked, 128), F32),
    ]
    return pl.pallas_call(
        kernel,
        in_specs=[whole()] * len(ins) + [far()],
        out_specs=[whole()] * len(outs),
        out_shape=outs,
        compiler_params=params(16),
        name="project",
    )(*ins, after)


def add_pieces(mine, received):
    count = mine.shape[0]

    def kernel(mine_ref, received_ref, *out_refs):
        for s in range(count):
            out_refs[s][...] = (mine_ref[s].astype(F32) + received_ref[s].astype(F32)).astype(BF)

    outs = [like(mine.shape[1:])] * count
    return pl.pallas_call(
        kernel,
        in_specs=[whole()] * 2,
        out_specs=[whole()] * len(outs),
        out_shape=outs,
        compiler_params=params(8),
        name="add_pieces",
    )(mine, received)


def touch(arrays, after):
    def kernel(*refs):
        refs[-1][...] = jnp.zeros_like(refs[-1])

    return pl.pallas_call(
        kernel,
        in_specs=[whole()] * len(arrays) + [far()],
        out_specs=whole(),
        out_shape=like((8, 128), F32),
        compiler_params=params(4),
        name="touch",
    )(*arrays, after)


def branch_share(pieces, w_out, parts, after):
    count = len(pieces)
    picked, both = pieces[0].shape
    half, part = both // 2, w_out.shape[1] // parts

    def kernel(*refs):
        piece_refs, out_w_ref = refs[:count], refs[count]
        total_ref, out_refs = refs[count + 2], refs[count + 3 :]
        tp = lax.axis_index("tp")
        total = piece_refs[0][...].astype(F32)
        for ref in piece_refs[1:]:
            total += ref[...].astype(F32)
        total_ref[...] = total.astype(BF)
        attended = total_ref[:, half:]
        for s in range(parts):
            columns = pl.ds(pl.multiple_of(lax.rem(tp + s, parts) * part, part), part)
            out_refs[s][...] = mm(attended, out_w_ref[:, columns], NN).astype(BF)

    return pl.pallas_call(
        kernel,
        in_specs=[whole()] * (count + 1) + [far()],
        out_specs=[whole()] * (1 + parts),
        out_shape=[like((picked, both))] + [like((picked, part))] * parts,
        compiler_params=params(16),
        cost_estimate=pl.CostEstimate(flops=10**9, bytes_accessed=2**22, transcendentals=0),
        name="branch_share",
    )(*pieces, w_out, after)


def hidden_share(total, kv_grads, in_pieces, own, w_query, w_key, w_value):
    parts = len(in_pieces)
    picked, part = in_pieces[0].shape
    half = w_query.shape[1]

    def kernel(total_ref, *refs):
        in_refs = refs[:parts]
        kv_ref, own_ref, query_ref, key_ref, value_ref = refs[parts : parts + 5]
        out_refs = refs[parts + 5 :]
        tp = lax.axis_index("tp")
        query_grad, attended = total_ref[:, :half], total_ref[:, half:]
        kv_sum = kv_ref[0].astype(F32)
        for b in range(1, kv_ref.shape[0]):
            kv_sum += kv_ref[b].astype(F32)
        kv_sum = kv_sum.astype(BF)
        key_grad, value_grad = kv_sum[:, :HEAD_DIM], kv_sum[:, HEAD_DIM:]
        stat = jnp.zeros((picked, 1), F32)
        for s in range(parts):
            rows = pl.ds(pl.multiple_of(lax.rem(tp + s, parts) * part, part), part)
            hidden = mm(query_grad, query_ref[rows, :], NT)
            hidden += mm(key_grad, key_ref[rows, :], NT)
            hidden += mm(value_grad, value_ref[rows, :], NT)
            rows_in = in_refs[(parts - s) % parts][...].astype(F32)
            stat += jnp.sum(hidden * rows_in, axis=1, keepdims=True)
            out_refs[s][:, :part] = hidden.astype(BF)
        stat = stat * (1.0 / (part * parts))
        grads = own_ref[:, half:].astype(F32)
        gate_sum = jnp.sum(attended.astype(F32) * grads, axis=1, keepdims=True)
        stat_high, gate_high = stat.astype(BF).astype(F32), gate_sum.astype(BF).astype(F32)
        lane = lax.broadcasted_iota(jnp.int32, (picked, 128), 1)
        extra = jnp.where(lane == 0, stat_high, 0.0)
        extra = jnp.where(lane == 1, gate_high, extra)
        extra = jnp.where(lane == 2, stat - stat_high, extra)
        extra = jnp.where(lane == 3, gate_sum - gate_high, extra).astype(BF)
        for s in range(parts):
            out_refs[s][:, part:] = extra

    ins = (total, *in_pieces, kv_grads, own, w_query, w_key, w_value)
    return pl.pallas_call(
        kernel,
        in_specs=[whole()] * len(ins),
        out_specs=[whole()] * parts,
        out_shape=[like((picked, part + 128))] * parts,
        compiler_params=params(16),
        cost_estimate=pl.CostEstimate(flops=2 * 10**10, bytes_accessed=2**26, transcendentals=0),
        name="hidden_share",
    )(*ins)


def put_block(base, spot, new, i, rows):
    row = lax.broadcasted_iota(jnp.int32, (rows, spot.shape[1]), 0)
    here = jnp.where(row + i * rows == spot, 1.0, 0.0)
    hit = jnp.max(here, axis=1, keepdims=True) > 0.5
    return jnp.where(hit, mm(here.astype(BF), new, NN), base.astype(F32)).astype(BF)


def put_rows(sizes, base, chosen, ins, rows_of, name):
    total, width = base.shape
    rows = min(128, total)
    steps = total // rows
    count = len(ins)

    def kernel(chosen_ref, base_ref, *refs):
        out_ref, block_ref, sems = refs[count:]
        new = rows_of(lax.axis_index("tp"), *refs[:count]).astype(BF)
        spot = chosen_ref[...] - my_first_row(sizes, total)
        started = []
        for i in range(steps):
            part = slice(i * rows, (i + 1) * rows)
            block_ref[part, :] = put_block(base_ref[part, :], spot, new, i, rows)
            copy = pltpu.make_async_copy(block_ref.at[part], out_ref.at[part], sems.at[i])
            copy.start()
            started.append(copy)
        for copy in started:
            copy.wait()

    return pl.pallas_call(
        kernel,
        in_specs=[whole()] * (2 + count),
        out_specs=far(),
        out_shape=like((total, width)),
        scratch_shapes=[pltpu.VMEM((total, width), BF), pltpu.SemaphoreType.DMA((steps,))],
        compiler_params=params(8),
        cost_estimate=pl.CostEstimate(flops=3 * 10**9, bytes_accessed=2**23, transcendentals=0),
        name=name,
    )(chosen, base, *ins)


def put_mixed(sizes, tokens, chosen, rows_in, branches, scales):
    def rows_of(tp, in_ref, scales_ref, *branch_refs):
        branch = branch_refs[0][...].astype(F32)
        for ref in branch_refs[1:]:
            branch += ref[...].astype(F32)
        return in_ref[...].astype(F32) + scales_ref[:, 0:1] * branch

    return put_rows(sizes, tokens, chosen, (rows_in, scales, *branches), rows_of, "put_mixed")


def put_grad(sizes, cotangent, chosen, rows_in, rows_grad, shares, scales, router):
    width = cotangent.shape[1]

    def rows_of(tp, in_ref, grad_ref, scales_ref, router_ref, *share_refs):
        gating, inverse_rows = scales_ref[:, 0:1], scales_ref[:, 1:2]
        wide_in = in_ref[...].astype(F32)
        summed = share_refs[0][...].astype(F32)
        for ref in share_refs[1:]:
            summed += ref[...].astype(F32)
        hidden, extra = summed[:, :width], summed[:, width:]
        row_stat = extra[:, 0:1] + extra[:, 2:3]
        logit_grad = (extra[:, 1:2] + extra[:, 3:4]) * (1.0 - gating)
        router_own = router_ref[:, pl.ds(pl.multiple_of(tp * width, width), width)].astype(F32)
        delta = inverse_rows * hidden - wide_in * (inverse_rows**3 * row_stat)
        delta = delta + logit_grad * router_own
        return grad_ref[...].astype(F32) + delta

    ins = (rows_in, rows_grad, scales, router, *shares)
    return put_rows(sizes, cotangent, chosen, ins, rows_of, "put_grad")


class Tiles:
    def __init__(self, picked, planes, columns, cores, heads):
        self.picked, self.planes, self.columns, self.cores, self.heads = (
            picked, planes, columns, cores, heads,
        )
        self.group = cores * picked
        self.lanes = heads * self.group
        self.keys = planes * picked
        self.half = heads * HEAD_DIM

    def fill(self, place, own, other, group_ref):
        core = place[2]
        mine = pl.ds(pl.multiple_of(core * self.picked, self.picked), self.picked)
        theirs = pl.ds(pl.multiple_of((1 - core) * self.picked, self.picked), self.picked)
        for s in range(self.columns):
            group_ref[s, mine, :] = own[s][...]
            group_ref[s, theirs, :] = other[s][...]

    def stacked(self, group_ref, s, first):
        parts = [
            group_ref[s, :, first + h * HEAD_DIM : first + (h + 1) * HEAD_DIM]
            for h in range(self.heads)
        ]
        return jnp.concatenate(parts, axis=0)

    def y_of(self, place, s):
        return lax.rem(place[1] + self.columns - s, self.columns)

    def scores(self, place, keys, queries, s):
        z, y, core = place[0], place[1], place[2]
        plane_rows = self.columns * self.group
        logits = mm(keys, queries, NT) * (LOG2E / math.sqrt(HEAD_DIM))
        key = lax.broadcasted_iota(jnp.int32, (self.keys, 1), 0)
        key_rank = (
            lax.div(key, self.picked) * plane_rows
            + (y * self.cores + core) * self.picked
            + lax.rem(key, self.picked)
        )
        lane = lax.broadcasted_iota(jnp.int32, (1, self.lanes), 1)
        query_rank = z * plane_rows + self.y_of(place, s) * self.group + lax.rem(lane, self.group)
        return jnp.where(key_rank <= query_rank, logits, FLOOR)


def softmax_parts(tiles, own, other, key_values):
    n = tiles.columns

    def kernel(kv_ref, *refs):
        own_refs, other_refs, out_ref, group_ref = refs[:n], refs[n : 2 * n], refs[2 * n], refs[-1]
        at = my_place()
        tiles.fill(at, own_refs, other_refs, group_ref)
        keys, values = kv_ref[:, :HEAD_DIM], kv_ref[:, HEAD_DIM:]
        for s in range(n):
            queries = tiles.stacked(group_ref, s, 0)
            grads = tiles.stacked(group_ref, s, tiles.half)
            logits = tiles.scores(at, keys, queries, s)
            top = jnp.max(logits, axis=0, keepdims=True)
            weights = jnp.exp2(logits - top)
            prob_grad = mm(values, grads, NT)
            total = jnp.sum(weights, axis=0, keepdims=True)
            inner = jnp.sum(weights * prob_grad, axis=0, keepdims=True)
            some = top > 0.5 * FLOOR
            slot = tiles.y_of(at, s)
            out_ref[slot, 0:1, :] = jnp.where(some, top + jnp.log(total) * LOG2E, FLOOR)
            out_ref[slot, 1:2, :] = jnp.where(some, inner / total, 0.0)

    return pl.pallas_call(
        kernel,
        in_specs=[whole()] * (1 + 2 * n),
        out_specs=whole(),
        out_shape=jax.ShapeDtypeStruct((n, 2, tiles.lanes), F32),
        scratch_shapes=[pltpu.VMEM((n, tiles.group, 2 * tiles.half), BF)],
        compiler_params=params(24),
        name="softmax_parts",
    )(key_values, *own, *other)


def attention_parts(tiles, own, other, key_values, parts):
    n = tiles.columns
    scale = 1.0 / math.sqrt(HEAD_DIM)

    def kernel(kv_ref, parts_ref, *refs):
        own_refs, other_refs = refs[:n], refs[n : 2 * n]
        mine_ref, theirs_ref, kv_grad_ref, group_ref, result_ref = refs[2 * n :]
        at = my_place()
        tiles.fill(at, own_refs, other_refs, group_ref)
        keys, values = kv_ref[:, :HEAD_DIM], kv_ref[:, HEAD_DIM:]
        keys_t, values_t = keys.T, values.T
        key_grad = jnp.zeros((tiles.keys, HEAD_DIM), F32)
        value_grad = jnp.zeros((tiles.keys, HEAD_DIM), F32)
        core = at[2]
        mine = pl.ds(pl.multiple_of(core * tiles.picked, tiles.picked), tiles.picked)
        theirs = pl.ds(pl.multiple_of((1 - core) * tiles.picked, tiles.picked), tiles.picked)
        for s in range(n):
            slot = tiles.y_of(at, s)
            tops = [parts_ref[b, slot, 0:1, :] for b in range(n * tiles.cores)]
            top = tops[0]
            for one in tops[1:]:
                top = jnp.maximum(top, one)
            total, inner = jnp.zeros_like(top), jnp.zeros_like(top)
            for b in range(n * tiles.cores):
                weight = jnp.exp2(tops[b] - top)
                total += weight
                inner += weight * parts_ref[b, slot, 1:2, :]
            shift = top + jnp.log(total) * LOG2E
            row_inner = inner / total
            queries = tiles.stacked(group_ref, s, 0)
            grads = tiles.stacked(group_ref, s, tiles.half)
            probs = jnp.exp2(tiles.scores(at, keys, queries, s) - shift)
            prob_grad = mm(values, grads, NT)
            score_low = (probs * (prob_grad - row_inner)).astype(BF)
            probs_low = probs.astype(BF)
            key_grad += mm(score_low, queries, NN)
            value_grad += mm(probs_low, grads, NN)
            query_t = mm(keys_t, score_low, NN) * scale
            output_t = mm(values_t, probs_low, NN)
            for h in range(tiles.heads):
                lanes = slice(h * tiles.group, (h + 1) * tiles.group)
                columns = slice(h * HEAD_DIM, (h + 1) * HEAD_DIM)
                shifted = slice(tiles.half + h * HEAD_DIM, tiles.half + (h + 1) * HEAD_DIM)
                result_ref[s, :, columns] = query_t[:, lanes].T.astype(BF)
                result_ref[s, :, shifted] = output_t[:, lanes].T.astype(BF)
            mine_ref[s, :, :] = result_ref[s, mine, :]
            theirs_ref[s, :, :] = result_ref[s, theirs, :]
        kv_grad_ref[:, :HEAD_DIM] = (key_grad * scale).astype(BF)
        kv_grad_ref[:, HEAD_DIM:] = value_grad.astype(BF)

    rows = like((n, tiles.picked, 2 * tiles.half))
    outs = [rows, rows, like((tiles.keys, 2 * HEAD_DIM))]
    return pl.pallas_call(
        kernel,
        in_specs=[whole()] * (2 + 2 * n),
        out_specs=[whole()] * 3,
        out_shape=outs,
        scratch_shapes=[pltpu.VMEM((n, tiles.group, 2 * tiles.half), BF)] * 2,
        compiler_params=params(24),
        name="attention_parts",
    )(key_values, parts, *own, *other)


def copies(array, count):
    return jnp.broadcast_to(array[None], (count,) + array.shape)


def exchange(array, axis):
    return lax.all_to_all(array, axis, 0, 0, tiled=True)


def shifted(array, axis, count, step):
    return lax.ppermute(array, axis, [(i, (i + step) % count) for i in range(count)])


def around_ring(piece, axis, count):
    pieces = [piece, shifted(piece, axis, count, 1)]
    if count == 2:
        return pieces
    last = shifted(piece, axis, count, count - 1)
    return pieces + [shifted(last, axis, count, count - 1), last]


def around_tp(shares, count):
    return [shares[0]] + [shifted(shares[s], "tp", count, s) for s in range(1, count)]


def on_device(sizes, tokens, chosen, router, w_query, w_key, w_value, w_out, cotangent):
    planes, columns, cores, parts_tp = sizes
    picked = chosen.shape[0]
    chosen, router = chosen[None, :], router[None, :]
    tiles = Tiles(picked, planes, columns, cores, w_query.shape[1] // HEAD_DIM)

    rows_grad = pick_rows(sizes, cotangent, chosen)
    grads = around_ring(rows_grad, "tp", parts_tp)
    rows_in = pick_rows(sizes, tokens, chosen)
    inputs = [rows_in] + [shifted(rows_in, "tp", parts_tp, s) for s in range(1, parts_tp)]
    near = touch((w_out, w_key, w_value), rows_in)
    key_values, mine, scales = project(
        sizes, inputs, grads, router, w_query, w_key, w_value, w_out, near
    )
    own = [mine] + [shifted(mine, "y", columns, s) for s in range(1, columns)]
    key_values = exchange(key_values, "z").reshape(tiles.keys, 2 * HEAD_DIM)
    key_values, *own = lax.optimization_barrier((key_values, *own))
    other = [shifted(piece, "core", cores, 1) for piece in own]
    parts = softmax_parts(tiles, own, other, key_values)
    parts = exchange(copies(parts, columns * cores), ("y", "core"))
    mine, theirs, kv_grads = attention_parts(tiles, own, other, key_values, parts)

    kv_grads = exchange(kv_grads.reshape(planes, picked, 2 * HEAD_DIM), "z")
    chip = add_pieces(mine, shifted(theirs, "core", cores, 1))
    pieces = [chip[0]] + [shifted(chip[s], "y", columns, columns - s) for s in range(1, columns)]
    total, *branches = branch_share(pieces, w_out, parts_tp, kv_grads)
    shares = hidden_share(total, kv_grads, inputs, own[0], w_query, w_key, w_value)
    branches = around_tp(branches, parts_tp)
    shares = around_tp(shares, parts_tp)
    mixed = put_mixed(sizes, tokens, chosen, rows_in, branches, scales)
    input_grad = put_grad(
        sizes, cotangent, chosen, rows_in, rows_grad, shares, scales, router
    )
    return mixed, input_grad


def solution(mesh):
    sizes = (8, 4, 2, 4)
    return build(mesh, sizes)


def build(mesh, sizes):
    fine = Mesh(mesh.devices.reshape(sizes), ("z", "y", "core", "tp"))
    ctx = ("z", "y", "core")

    def step(*arrays):
        return on_device(sizes, *arrays)

    placed = (
        P(ctx, "tp"), P(ctx), P(), P(None, "tp"), P(None, "tp"), P(None, "tp"), P("tp", None), P(ctx, "tp"),
    )
    return jax.shard_map(
        step,
        mesh=fine,
        in_specs=placed,
        out_specs=(P(ctx, "tp"), P(ctx, "tp")),
        check_vma=False,
    )
```

```python
import math

import jax
import jax.numpy as jnp
from jax import lax
from jax.experimental import pallas as pl
from jax.experimental.pallas import tpu as pltpu
from jax.sharding import Mesh
from jax.sharding import PartitionSpec as P

HEAD_DIM = 128
EPS = 1e-05
FLOOR = -1e30
LOG2E = 1.0 / math.log(2.0)
BF = jnp.bfloat16
F32 = jnp.float32
VMEM = pltpu.VMEM
NT = (((1,), (1,)), ((), ()))
NN = (((1,), (0,)), ((), ()))


def mm(left, right, dims):
    return lax.dot_general(left, right, dims, preferred_element_type=F32)


def whole():
    return pl.BlockSpec(memory_space=VMEM)


def far():
    return pl.BlockSpec(memory_space=pl.ANY)


def like(shape, dtype=BF):
    return jax.ShapeDtypeStruct(tuple(shape), dtype)


def params(mib):
    return pltpu.CompilerParams(vmem_limit_bytes=mib * 2**20)


def my_place():
    return lax.axis_index("z"), lax.axis_index("y"), lax.axis_index("core")


def my_first_row(sizes, tok_rows):
    z, y, core = my_place()
    return ((z * sizes[1] + y) * sizes[2] + core) * tok_rows


def pick_rows(sizes, array, chosen):
    picked = chosen.shape[1]
    total, width = array.shape
    rows = min(256, total)

    def kernel(chosen_ref, array_ref, out_ref):
        square = (picked, picked)
        eye = lax.broadcasted_iota(jnp.int32, square, 0) == lax.broadcasted_iota(jnp.int32, square, 1)
        local = (chosen_ref[...] - my_first_row(sizes, total)).astype(F32)
        spot = jnp.sum(jnp.where(eye, jnp.broadcast_to(local, square), 0.0), axis=1, keepdims=True)
        column = lax.broadcasted_iota(jnp.int32, (picked, total), 1)
        here = jnp.where(column == spot.astype(jnp.int32), 1.0, 0.0).astype(BF)
        out_ref[...] = mm(here, array_ref[...], NN).astype(BF)

    return pl.pallas_call(
        kernel,
        in_specs=[whole()] * 2,
        out_specs=whole(),
        out_shape=like((picked, width)),
        compiler_params=params(8),
        name="pick_rows",
    )(chosen, array)


def project(sizes, in_pieces, grad_pieces, router, w_query, w_key, w_value, w_out, after):
    parts = len(in_pieces)
    picked, part = in_pieces[0].shape
    width = part * parts
    half = w_query.shape[1]

    def kernel(*refs):
        in_refs, grad_refs = refs[:parts], refs[parts : 2 * parts]
        router_ref, query_ref, key_ref, value_ref, out_w_ref = refs[2 * parts : 2 * parts + 5]
        kv_ref, own_ref, scales_ref = refs[2 * parts + 6 :]
        tp = lax.axis_index("tp")

        def span(s):
            owner = lax.rem(tp + parts - s, parts)
            return pl.ds(pl.multiple_of(owner * part, part), part)

        squares = jnp.zeros((picked, 1), F32)
        logit = jnp.zeros((picked, 1), F32)
        for s in range(parts):
            rows = in_refs[s][...].astype(F32)
            squares += jnp.sum(rows * rows, axis=1, keepdims=True)
            weights = router_ref[:, span(s)].astype(F32)
            logit += jnp.sum(rows * weights, axis=1, keepdims=True)
        inverse = lax.rsqrt(squares * (1.0 / width) + EPS)
        gate = 1.0 / (1.0 + jnp.exp(-logit))
        lane = lax.broadcasted_iota(jnp.int32, (picked, 128), 1)
        scales_ref[...] = jnp.where(lane == 0, gate, inverse)
        keys = jnp.zeros((picked, HEAD_DIM), F32)
        values = jnp.zeros((picked, HEAD_DIM), F32)
        queries = jnp.zeros((picked, half), F32)
        grads = jnp.zeros((picked, half), F32)
        for s in range(parts):
            rows = span(s)
            normed = (in_refs[s][...].astype(F32) * inverse).astype(BF)
            keys += mm(normed, key_ref[rows, :], NN)
            values += mm(normed, value_ref[rows, :], NN)
            queries += mm(normed, query_ref[rows, :], NN)
            grads += mm(grad_refs[s][...], out_w_ref[:, rows], NT)
        own_ref[:, :half] = queries.astype(BF)
        own_ref[:, half:] = (gate * grads).astype(BF)
        low = jnp.concatenate([keys, values], axis=1).astype(BF)
        for b in range(sizes[0]):
            kv_ref[b] = low

    ins = (*in_pieces, *grad_pieces, router, w_query, w_key, w_value, w_out)
    outs = [
        like((sizes[0], picked, 2 * HEAD_DIM)),
        like((picked, 2 * half)),
        like((picked, 128), F32),
    ]
    return pl.pallas_call(
        kernel,
        in_specs=[whole()] * len(ins) + [far()],
        out_specs=[whole()] * len(outs),
        out_shape=outs,
        compiler_params=params(16),
        name="project",
    )(*ins, after)


def add_pieces(mine, received):
    count = mine.shape[0]

    def kernel(mine_ref, received_ref, *out_refs):
        for s in range(count):
            out_refs[s][...] = (mine_ref[s].astype(F32) + received_ref[s].astype(F32)).astype(BF)

    outs = [like(mine.shape[1:])] * count
    return pl.pallas_call(
        kernel,
        in_specs=[whole()] * 2,
        out_specs=[whole()] * len(outs),
        out_shape=outs,
        compiler_params=params(8),
        name="add_pieces",
    )(mine, received)


def touch(arrays, after):
    def kernel(*refs):
        refs[-1][...] = jnp.zeros_like(refs[-1])

    return pl.pallas_call(
        kernel,
        in_specs=[whole()] * len(arrays) + [far()],
        out_specs=whole(),
        out_shape=like((8, 128), F32),
        compiler_params=params(4),
        name="touch",
    )(*arrays, after)


def branch_share(pieces, w_out, parts, after):
    count = len(pieces)
    picked, both = pieces[0].shape
    half, part = both // 2, w_out.shape[1] // parts

    def kernel(*refs):
        piece_refs, out_w_ref = refs[:count], refs[count]
        total_ref, out_refs = refs[count + 2], refs[count + 3 :]
        tp = lax.axis_index("tp")
        total = piece_refs[0][...].astype(F32)
        for ref in piece_refs[1:]:
            total += ref[...].astype(F32)
        total_ref[...] = total.astype(BF)
        attended = total_ref[:, half:]
        for s in range(parts):
            columns = pl.ds(pl.multiple_of(lax.rem(tp + s, parts) * part, part), part)
            out_refs[s][...] = mm(attended, out_w_ref[:, columns], NN).astype(BF)

    return pl.pallas_call(
        kernel,
        in_specs=[whole()] * (count + 1) + [far()],
        out_specs=[whole()] * (1 + parts),
        out_shape=[like((picked, both))] + [like((picked, part))] * parts,
        compiler_params=params(16),
        cost_estimate=pl.CostEstimate(flops=2 * 10**10, bytes_accessed=2**26, transcendentals=0),
        name="branch_share",
    )(*pieces, w_out, after)


def hidden_share(total, kv_grads, in_pieces, own, w_query, w_key, w_value):
    parts = len(in_pieces)
    picked, part = in_pieces[0].shape
    half = w_query.shape[1]

    def kernel(total_ref, *refs):
        in_refs = refs[:parts]
        kv_ref, own_ref, query_ref, key_ref, value_ref = refs[parts : parts + 5]
        out_refs = refs[parts + 5 :]
        tp = lax.axis_index("tp")
        query_grad, attended = total_ref[:, :half], total_ref[:, half:]
        kv_sum = kv_ref[0].astype(F32)
        for b in range(1, kv_ref.shape[0]):
            kv_sum += kv_ref[b].astype(F32)
        kv_sum = kv_sum.astype(BF)
        key_grad, value_grad = kv_sum[:, :HEAD_DIM], kv_sum[:, HEAD_DIM:]
        stat = jnp.zeros((picked, 1), F32)
        for s in range(parts):
            rows = pl.ds(pl.multiple_of(lax.rem(tp + s, parts) * part, part), part)
            hidden = mm(query_grad, query_ref[rows, :], NT)
            hidden += mm(key_grad, key_ref[rows, :], NT)
            hidden += mm(value_grad, value_ref[rows, :], NT)
            rows_in = in_refs[(parts - s) % parts][...].astype(F32)
            stat += jnp.sum(hidden * rows_in, axis=1, keepdims=True)
            out_refs[s][:, :part] = hidden.astype(BF)
        stat = stat * (1.0 / (part * parts))
        grads = own_ref[:, half:].astype(F32)
        gate_sum = jnp.sum(attended.astype(F32) * grads, axis=1, keepdims=True)
        stat_high, gate_high = stat.astype(BF).astype(F32), gate_sum.astype(BF).astype(F32)
        lane = lax.broadcasted_iota(jnp.int32, (picked, 128), 1)
        extra = jnp.where(lane == 0, stat_high, 0.0)
        extra = jnp.where(lane == 1, gate_high, extra)
        extra = jnp.where(lane == 2, stat - stat_high, extra)
        extra = jnp.where(lane == 3, gate_sum - gate_high, extra).astype(BF)
        for s in range(parts):
            out_refs[s][:, part:] = extra

    ins = (total, *in_pieces, kv_grads, own, w_query, w_key, w_value)
    return pl.pallas_call(
        kernel,
        in_specs=[whole()] * len(ins),
        out_specs=[whole()] * parts,
        out_shape=[like((picked, part + 128))] * parts,
        compiler_params=params(16),
        cost_estimate=pl.CostEstimate(flops=2 * 10**10, bytes_accessed=2**26, transcendentals=0),
        name="hidden_share",
    )(*ins)


def put_block(base, spot, new, i, rows):
    row = lax.broadcasted_iota(jnp.int32, (rows, spot.shape[1]), 0)
    here = jnp.where(row + i * rows == spot, 1.0, 0.0)
    hit = jnp.max(here, axis=1, keepdims=True) > 0.5
    return jnp.where(hit, mm(here.astype(BF), new, NN), base.astype(F32)).astype(BF)


def put_rows(sizes, base, chosen, ins, rows_of, name):
    total, width = base.shape
    rows = min(128, total)
    steps = total // rows
    count = len(ins)

    def kernel(chosen_ref, base_ref, *refs):
        out_ref, block_ref, sems = refs[count:]
        new = rows_of(lax.axis_index("tp"), *refs[:count]).astype(BF)
        spot = chosen_ref[...] - my_first_row(sizes, total)
        started = []
        for i in range(steps):
            part = slice(i * rows, (i + 1) * rows)
            block_ref[part, :] = put_block(base_ref[part, :], spot, new, i, rows)
            copy = pltpu.make_async_copy(block_ref.at[part], out_ref.at[part], sems.at[i])
            copy.start()
            started.append(copy)
        for copy in started:
            copy.wait()

    return pl.pallas_call(
        kernel,
        in_specs=[whole()] * (2 + count),
        out_specs=far(),
        out_shape=like((total, width)),
        scratch_shapes=[pltpu.VMEM((total, width), BF), pltpu.SemaphoreType.DMA((steps,))],
        compiler_params=params(8),
        cost_estimate=pl.CostEstimate(flops=3 * 10**9, bytes_accessed=2**23, transcendentals=0),
        name=name,
    )(chosen, base, *ins)


def put_mixed(sizes, tokens, chosen, rows_in, branches, scales):
    def rows_of(tp, in_ref, scales_ref, *branch_refs):
        branch = branch_refs[0][...].astype(F32)
        for ref in branch_refs[1:]:
            branch += ref[...].astype(F32)
        return in_ref[...].astype(F32) + scales_ref[:, 0:1] * branch

    return put_rows(sizes, tokens, chosen, (rows_in, scales, *branches), rows_of, "put_mixed")


def put_grad(sizes, cotangent, chosen, rows_in, rows_grad, shares, scales, router):
    width = cotangent.shape[1]

    def rows_of(tp, in_ref, grad_ref, scales_ref, router_ref, *share_refs):
        gating, inverse_rows = scales_ref[:, 0:1], scales_ref[:, 1:2]
        wide_in = in_ref[...].astype(F32)
        summed = share_refs[0][...].astype(F32)
        for ref in share_refs[1:]:
            summed += ref[...].astype(F32)
        hidden, extra = summed[:, :width], summed[:, width:]
        row_stat = extra[:, 0:1] + extra[:, 2:3]
        logit_grad = (extra[:, 1:2] + extra[:, 3:4]) * (1.0 - gating)
        router_own = router_ref[:, pl.ds(pl.multiple_of(tp * width, width), width)].astype(F32)
        delta = inverse_rows * hidden - wide_in * (inverse_rows**3 * row_stat)
        delta = delta + logit_grad * router_own
        return grad_ref[...].astype(F32) + delta

    ins = (rows_in, rows_grad, scales, router, *shares)
    return put_rows(sizes, cotangent, chosen, ins, rows_of, "put_grad")


class Tiles:
    def __init__(self, picked, planes, columns, cores, heads):
        self.picked, self.planes, self.columns, self.cores, self.heads = (
            picked, planes, columns, cores, heads,
        )
        self.group = cores * picked
        self.lanes = heads * self.group
        self.keys = planes * picked
        self.half = heads * HEAD_DIM

    def fill(self, place, own, other, group_ref):
        core = place[2]
        mine = pl.ds(pl.multiple_of(core * self.picked, self.picked), self.picked)
        theirs = pl.ds(pl.multiple_of((1 - core) * self.picked, self.picked), self.picked)
        for s in range(self.columns):
            group_ref[s, mine, :] = own[s][...]
            group_ref[s, theirs, :] = other[s][...]

    def stacked(self, group_ref, s, first):
        parts = [
            group_ref[s, :, first + h * HEAD_DIM : first + (h + 1) * HEAD_DIM]
            for h in range(self.heads)
        ]
        return jnp.concatenate(parts, axis=0)

    def y_of(self, place, s):
        return lax.rem(place[1] + self.columns - s, self.columns)

    def scores(self, place, keys, queries, s):
        z, y, core = place[0], place[1], place[2]
        plane_rows = self.columns * self.group
        logits = mm(keys, queries, NT) * (LOG2E / math.sqrt(HEAD_DIM))
        key = lax.broadcasted_iota(jnp.int32, (self.keys, 1), 0)
        key_rank = (
            lax.div(key, self.picked) * plane_rows
            + (y * self.cores + core) * self.picked
            + lax.rem(key, self.picked)
        )
        lane = lax.broadcasted_iota(jnp.int32, (1, self.lanes), 1)
        query_rank = z * plane_rows + self.y_of(place, s) * self.group + lax.rem(lane, self.group)
        return jnp.where(key_rank <= query_rank, logits, FLOOR)


def softmax_parts(tiles, own, other, key_values):
    n = tiles.columns

    def kernel(kv_ref, *refs):
        own_refs, other_refs, out_ref, group_ref = refs[:n], refs[n : 2 * n], refs[2 * n], refs[-1]
        at = my_place()
        tiles.fill(at, own_refs, other_refs, group_ref)
        keys, values = kv_ref[:, :HEAD_DIM], kv_ref[:, HEAD_DIM:]
        for s in range(n):
            queries = tiles.stacked(group_ref, s, 0)
            grads = tiles.stacked(group_ref, s, tiles.half)
            logits = tiles.scores(at, keys, queries, s)
            top = jnp.max(logits, axis=0, keepdims=True)
            weights = jnp.exp2(logits - top)
            prob_grad = mm(values, grads, NT)
            total = jnp.sum(weights, axis=0, keepdims=True)
            inner = jnp.sum(weights * prob_grad, axis=0, keepdims=True)
            some = top > 0.5 * FLOOR
            slot = tiles.y_of(at, s)
            out_ref[slot, 0:1, :] = jnp.where(some, top + jnp.log(total) * LOG2E, FLOOR)
            out_ref[slot, 1:2, :] = jnp.where(some, inner / total, 0.0)

    return pl.pallas_call(
        kernel,
        in_specs=[whole()] * (1 + 2 * n),
        out_specs=whole(),
        out_shape=jax.ShapeDtypeStruct((n, 2, tiles.lanes), F32),
        scratch_shapes=[pltpu.VMEM((n, tiles.group, 2 * tiles.half), BF)],
        compiler_params=params(24),
        name="softmax_parts",
    )(key_values, *own, *other)


def attention_parts(tiles, own, other, key_values, parts):
    n = tiles.columns
    scale = 1.0 / math.sqrt(HEAD_DIM)

    def kernel(kv_ref, parts_ref, *refs):
        own_refs, other_refs = refs[:n], refs[n : 2 * n]
        mine_ref, theirs_ref, kv_grad_ref, group_ref, result_ref = refs[2 * n :]
        at = my_place()
        tiles.fill(at, own_refs, other_refs, group_ref)
        keys, values = kv_ref[:, :HEAD_DIM], kv_ref[:, HEAD_DIM:]
        keys_t, values_t = keys.T, values.T
        key_grad = jnp.zeros((tiles.keys, HEAD_DIM), F32)
        value_grad = jnp.zeros((tiles.keys, HEAD_DIM), F32)
        core = at[2]
        mine = pl.ds(pl.multiple_of(core * tiles.picked, tiles.picked), tiles.picked)
        theirs = pl.ds(pl.multiple_of((1 - core) * tiles.picked, tiles.picked), tiles.picked)
        for s in range(n):
            slot = tiles.y_of(at, s)
            tops = [parts_ref[b, slot, 0:1, :] for b in range(n * tiles.cores)]
            top = tops[0]
            for one in tops[1:]:
                top = jnp.maximum(top, one)
            total, inner = jnp.zeros_like(top), jnp.zeros_like(top)
            for b in range(n * tiles.cores):
                weight = jnp.exp2(tops[b] - top)
                total += weight
                inner += weight * parts_ref[b, slot, 1:2, :]
            shift = top + jnp.log(total) * LOG2E
            row_inner = inner / total
            queries = tiles.stacked(group_ref, s, 0)
            grads = tiles.stacked(group_ref, s, tiles.half)
            probs = jnp.exp2(tiles.scores(at, keys, queries, s) - shift)
            prob_grad = mm(values, grads, NT)
            score_low = (probs * (prob_grad - row_inner)).astype(BF)
            probs_low = probs.astype(BF)
            key_grad += mm(score_low, queries, NN)
            value_grad += mm(probs_low, grads, NN)
            query_t = mm(keys_t, score_low, NN) * scale
            output_t = mm(values_t, probs_low, NN)
            for h in range(tiles.heads):
                lanes = slice(h * tiles.group, (h + 1) * tiles.group)
                columns = slice(h * HEAD_DIM, (h + 1) * HEAD_DIM)
                shifted = slice(tiles.half + h * HEAD_DIM, tiles.half + (h + 1) * HEAD_DIM)
                result_ref[s, :, columns] = query_t[:, lanes].T.astype(BF)
                result_ref[s, :, shifted] = output_t[:, lanes].T.astype(BF)
            mine_ref[s, :, :] = result_ref[s, mine, :]
            theirs_ref[s, :, :] = result_ref[s, theirs, :]
        kv_grad_ref[:, :HEAD_DIM] = (key_grad * scale).astype(BF)
        kv_grad_ref[:, HEAD_DIM:] = value_grad.astype(BF)

    rows = like((n, tiles.picked, 2 * tiles.half))
    outs = [rows, rows, like((tiles.keys, 2 * HEAD_DIM))]
    return pl.pallas_call(
        kernel,
        in_specs=[whole()] * (2 + 2 * n),
        out_specs=[whole()] * 3,
        out_shape=outs,
        scratch_shapes=[pltpu.VMEM((n, tiles.group, 2 * tiles.half), BF)] * 2,
        compiler_params=params(24),
        name="attention_parts",
    )(key_values, parts, *own, *other)


def copies(array, count):
    return jnp.broadcast_to(array[None], (count,) + array.shape)


def exchange(array, axis):
    return lax.all_to_all(array, axis, 0, 0, tiled=True)


def shifted(array, axis, count, step):
    return lax.ppermute(array, axis, [(i, (i + step) % count) for i in range(count)])


def around_ring(piece, axis, count):
    pieces = [piece, shifted(piece, axis, count, 1)]
    if count == 2:
        return pieces
    last = shifted(piece, axis, count, count - 1)
    return pieces + [shifted(last, axis, count, count - 1), last]


def around_tp(shares, count):
    return [shares[0]] + [shifted(shares[s], "tp", count, s) for s in range(1, count)]


def on_device(sizes, tokens, chosen, router, w_query, w_key, w_value, w_out, cotangent):
    planes, columns, cores, parts_tp = sizes
    picked = chosen.shape[0]
    chosen, router = chosen[None, :], router[None, :]
    tiles = Tiles(picked, planes, columns, cores, w_query.shape[1] // HEAD_DIM)

    rows_grad = pick_rows(sizes, cotangent, chosen)
    grads = around_ring(rows_grad, "tp", parts_tp)
    rows_in = pick_rows(sizes, tokens, chosen)
    inputs = [rows_in] + [shifted(rows_in, "tp", parts_tp, s) for s in range(1, parts_tp)]
    near = touch((w_out, w_key, w_value), rows_in)
    key_values, mine, scales = project(
        sizes, inputs, grads, router, w_query, w_key, w_value, w_out, near
    )
    own = [mine] + [shifted(mine, "y", columns, s) for s in range(1, columns)]
    key_values = exchange(key_values, "z").reshape(tiles.keys, 2 * HEAD_DIM)
    key_values, *own = lax.optimization_barrier((key_values, *own))
    other = [shifted(piece, "core", cores, 1) for piece in own]
    parts = softmax_parts(tiles, own, other, key_values)
    parts = exchange(copies(parts, columns * cores), ("y", "core"))
    mine, theirs, kv_grads = attention_parts(tiles, own, other, key_values, parts)

    kv_grads = exchange(kv_grads.reshape(planes, picked, 2 * HEAD_DIM), "z")
    chip = add_pieces(mine, shifted(theirs, "core", cores, 1))
    pieces = [chip[0]] + [shifted(chip[s], "y", columns, columns - s) for s in range(1, columns)]
    total, *branches = branch_share(pieces, w_out, parts_tp, chip[0])
    shares = hidden_share(total, kv_grads, inputs, own[0], w_query, w_key, w_value)
    branches = around_tp(branches, parts_tp)
    shares = around_tp(shares, parts_tp)
    mixed = put_mixed(sizes, tokens, chosen, rows_in, branches, scales)
    input_grad = put_grad(
        sizes, cotangent, chosen, rows_in, rows_grad, shares, scales, router
    )
    return mixed, input_grad


def solution(mesh):
    sizes = (8, 4, 2, 4)
    return build(mesh, sizes)


def build(mesh, sizes):
    fine = Mesh(mesh.devices.reshape(sizes), ("z", "y", "core", "tp"))
    ctx = ("z", "y", "core")

    def step(*arrays):
        return on_device(sizes, *arrays)

    placed = (
        P(ctx, "tp"), P(ctx), P(), P(None, "tp"), P(None, "tp"), P(None, "tp"), P("tp", None), P(ctx, "tp"),
    )
    return jax.shard_map(
        step,
        mesh=fine,
        in_specs=placed,
        out_specs=(P(ctx, "tp"), P(ctx, "tp")),
        check_vma=False,
    )
```

```python
import math

import jax
import jax.numpy as jnp
from jax import lax
from jax.experimental import pallas as pl
from jax.experimental.pallas import tpu as pltpu
from jax.sharding import Mesh
from jax.sharding import PartitionSpec as P

HEAD_DIM = 128
EPS = 1e-05
FLOOR = -1e30
LOG2E = 1.0 / math.log(2.0)
BF = jnp.bfloat16
F32 = jnp.float32
VMEM = pltpu.VMEM
NT = (((1,), (1,)), ((), ()))
NN = (((1,), (0,)), ((), ()))


def mm(left, right, dims):
    return lax.dot_general(left, right, dims, preferred_element_type=F32)


def whole():
    return pl.BlockSpec(memory_space=VMEM)


def far():
    return pl.BlockSpec(memory_space=pl.ANY)


def like(shape, dtype=BF):
    return jax.ShapeDtypeStruct(tuple(shape), dtype)


def params(mib):
    return pltpu.CompilerParams(vmem_limit_bytes=mib * 2**20)


def my_place():
    return lax.axis_index("z"), lax.axis_index("y"), lax.axis_index("core")


def my_first_row(sizes, tok_rows):
    z, y, core = my_place()
    return ((z * sizes[1] + y) * sizes[2] + core) * tok_rows


def pick_rows(sizes, array, chosen):
    picked = chosen.shape[1]
    total, width = array.shape
    rows = min(256, total)

    def kernel(chosen_ref, array_ref, out_ref):
        square = (picked, picked)
        eye = lax.broadcasted_iota(jnp.int32, square, 0) == lax.broadcasted_iota(jnp.int32, square, 1)
        local = (chosen_ref[...] - my_first_row(sizes, total)).astype(F32)
        spot = jnp.sum(jnp.where(eye, jnp.broadcast_to(local, square), 0.0), axis=1, keepdims=True)
        column = lax.broadcasted_iota(jnp.int32, (picked, total), 1)
        here = jnp.where(column == spot.astype(jnp.int32), 1.0, 0.0).astype(BF)
        out_ref[...] = mm(here, array_ref[...], NN).astype(BF)

    return pl.pallas_call(
        kernel,
        in_specs=[whole()] * 2,
        out_specs=whole(),
        out_shape=like((picked, width)),
        compiler_params=params(8),
        name="pick_rows",
    )(chosen, array)


def project(sizes, in_pieces, grad_pieces, router, w_query, w_key, w_value, w_out, after):
    parts = len(in_pieces)
    picked, part = in_pieces[0].shape
    width = part * parts
    half = w_query.shape[1]

    def kernel(*refs):
        in_refs, grad_refs = refs[:parts], refs[parts : 2 * parts]
        router_ref, query_ref, key_ref, value_ref, out_w_ref = refs[2 * parts : 2 * parts + 5]
        kv_ref, own_ref, scales_ref = refs[2 * parts + 6 :]
        tp = lax.axis_index("tp")

        def span(s):
            owner = lax.rem(tp + parts - s, parts)
            return pl.ds(pl.multiple_of(owner * part, part), part)

        squares = jnp.zeros((picked, 1), F32)
        logit = jnp.zeros((picked, 1), F32)
        for s in range(parts):
            rows = in_refs[s][...].astype(F32)
            squares += jnp.sum(rows * rows, axis=1, keepdims=True)
            weights = router_ref[:, span(s)].astype(F32)
            logit += jnp.sum(rows * weights, axis=1, keepdims=True)
        inverse = lax.rsqrt(squares * (1.0 / width) + EPS)
        gate = 1.0 / (1.0 + jnp.exp(-logit))
        lane = lax.broadcasted_iota(jnp.int32, (picked, 128), 1)
        scales_ref[...] = jnp.where(lane == 0, gate, inverse)
        keys = jnp.zeros((picked, HEAD_DIM), F32)
        values = jnp.zeros((picked, HEAD_DIM), F32)
        queries = jnp.zeros((picked, half), F32)
        grads = jnp.zeros((picked, half), F32)
        for s in range(parts):
            rows = span(s)
            normed = (in_refs[s][...].astype(F32) * inverse).astype(BF)
            keys += mm(normed, key_ref[rows, :], NN)
            values += mm(normed, value_ref[rows, :], NN)
            queries += mm(normed, query_ref[rows, :], NN)
            grads += mm(grad_refs[s][...], out_w_ref[:, rows], NT)
        own_ref[:, :half] = queries.astype(BF)
        own_ref[:, half:] = (gate * grads).astype(BF)
        low = jnp.concatenate([keys, values], axis=1).astype(BF)
        for b in range(sizes[0]):
            kv_ref[b] = low

    ins = (*in_pieces, *grad_pieces, router, w_query, w_key, w_value, w_out)
    outs = [
        like((sizes[0], picked, 2 * HEAD_DIM)),
        like((picked, 2 * half)),
        like((picked, 128), F32),
    ]
    return pl.pallas_call(
        kernel,
        in_specs=[whole()] * len(ins) + [far()],
        out_specs=[whole()] * len(outs),
        out_shape=outs,
        compiler_params=params(16),
        name="project",
    )(*ins, after)


def add_pieces(mine, received):
    count = mine.shape[0]

    def kernel(mine_ref, received_ref, *out_refs):
        for s in range(count):
            out_refs[s][...] = (mine_ref[s].astype(F32) + received_ref[s].astype(F32)).astype(BF)

    outs = [like(mine.shape[1:])] * count
    return pl.pallas_call(
        kernel,
        in_specs=[whole()] * 2,
        out_specs=[whole()] * len(outs),
        out_shape=outs,
        compiler_params=params(8),
        name="add_pieces",
    )(mine, received)


def touch(arrays, after):
    def kernel(*refs):
        refs[-1][...] = jnp.zeros_like(refs[-1])

    return pl.pallas_call(
        kernel,
        in_specs=[whole()] * len(arrays) + [far()],
        out_specs=whole(),
        out_shape=like((8, 128), F32),
        compiler_params=params(4),
        name="touch",
    )(*arrays, after)


def branch_share(pieces, w_out, parts, after):
    count = len(pieces)
    picked, both = pieces[0].shape
    half, part = both // 2, w_out.shape[1] // parts

    def kernel(*refs):
        piece_refs, out_w_ref = refs[:count], refs[count]
        total_ref, out_refs = refs[count + 2], refs[count + 2 :]
        tp = lax.axis_index("tp")
        total = piece_refs[0][...].astype(F32)
        for ref in piece_refs[1:]:
            total += ref[...].astype(F32)
        total = total.astype(BF)
        total_ref[:, :both] = total
        attended = total[:, half:]
        for s in range(parts):
            columns = pl.ds(pl.multiple_of(lax.rem(tp + s, parts) * part, part), part)
            branch = mm(attended, out_w_ref[:, columns], NN).astype(BF)
            if s == 0:
                total_ref[:, both:] = branch
            else:
                out_refs[s][...] = branch

    return pl.pallas_call(
        kernel,
        in_specs=[whole()] * (count + 1) + [far()],
        out_specs=[whole()] * parts,
        out_shape=[like((picked, both + part))] + [like((picked, part))] * (parts - 1),
        compiler_params=params(16),
        cost_estimate=pl.CostEstimate(flops=2 * 10**10, bytes_accessed=2**26, transcendentals=0),
        name="branch_share",
    )(*pieces, w_out, after)


def hidden_share(total, kv_grads, in_pieces, own, w_query, w_key, w_value):
    parts = len(in_pieces)
    picked, part = in_pieces[0].shape
    half = w_query.shape[1]

    def kernel(total_ref, *refs):
        in_refs = refs[:parts]
        kv_ref, own_ref, query_ref, key_ref, value_ref = refs[parts : parts + 5]
        out_refs = refs[parts + 5 :]
        tp = lax.axis_index("tp")
        query_grad, attended = total_ref[:, :half], total_ref[:, half : 2 * half]
        kv_sum = kv_ref[0].astype(F32)
        for b in range(1, kv_ref.shape[0]):
            kv_sum += kv_ref[b].astype(F32)
        kv_sum = kv_sum.astype(BF)
        key_grad, value_grad = kv_sum[:, :HEAD_DIM], kv_sum[:, HEAD_DIM:]
        stat = jnp.zeros((picked, 1), F32)
        for s in range(parts):
            rows = pl.ds(pl.multiple_of(lax.rem(tp + s, parts) * part, part), part)
            hidden = mm(query_grad, query_ref[rows, :], NT)
            hidden += mm(key_grad, key_ref[rows, :], NT)
            hidden += mm(value_grad, value_ref[rows, :], NT)
            rows_in = in_refs[(parts - s) % parts][...].astype(F32)
            stat += jnp.sum(hidden * rows_in, axis=1, keepdims=True)
            out_refs[s][:, :part] = hidden.astype(BF)
        stat = stat * (1.0 / (part * parts))
        grads = own_ref[:, half:].astype(F32)
        gate_sum = jnp.sum(attended.astype(F32) * grads, axis=1, keepdims=True)
        stat_high, gate_high = stat.astype(BF).astype(F32), gate_sum.astype(BF).astype(F32)
        lane = lax.broadcasted_iota(jnp.int32, (picked, 128), 1)
        extra = jnp.where(lane == 0, stat_high, 0.0)
        extra = jnp.where(lane == 1, gate_high, extra)
        extra = jnp.where(lane == 2, stat - stat_high, extra)
        extra = jnp.where(lane == 3, gate_sum - gate_high, extra).astype(BF)
        for s in range(parts):
            out_refs[s][:, part:] = extra

    ins = (total, *in_pieces, kv_grads, own, w_query, w_key, w_value)
    return pl.pallas_call(
        kernel,
        in_specs=[whole()] * len(ins),
        out_specs=[whole()] * parts,
        out_shape=[like((picked, part + 128))] * parts,
        compiler_params=params(16),
        cost_estimate=pl.CostEstimate(flops=2 * 10**10, bytes_accessed=2**26, transcendentals=0),
        name="hidden_share",
    )(*ins)


def put_block(base, spot, new, i, rows):
    row = lax.broadcasted_iota(jnp.int32, (rows, spot.shape[1]), 0)
    here = jnp.where(row + i * rows == spot, 1.0, 0.0)
    hit = jnp.max(here, axis=1, keepdims=True) > 0.5
    return jnp.where(hit, mm(here.astype(BF), new, NN), base.astype(F32)).astype(BF)


def put_rows(sizes, base, chosen, ins, rows_of, name):
    total, width = base.shape
    rows = min(128, total)
    steps = total // rows
    count = len(ins)

    def kernel(chosen_ref, base_ref, *refs):
        out_ref, block_ref, sems = refs[count:]
        new = rows_of(lax.axis_index("tp"), *refs[:count]).astype(BF)
        spot = chosen_ref[...] - my_first_row(sizes, total)
        started = []
        for i in range(steps):
            part = slice(i * rows, (i + 1) * rows)
            block_ref[part, :] = put_block(base_ref[part, :], spot, new, i, rows)
            copy = pltpu.make_async_copy(block_ref.at[part], out_ref.at[part], sems.at[i])
            copy.start()
            started.append(copy)
        for copy in started:
            copy.wait()

    return pl.pallas_call(
        kernel,
        in_specs=[whole()] * (2 + count),
        out_specs=far(),
        out_shape=like((total, width)),
        scratch_shapes=[pltpu.VMEM((total, width), BF), pltpu.SemaphoreType.DMA((steps,))],
        compiler_params=params(8),
        cost_estimate=pl.CostEstimate(flops=3 * 10**9, bytes_accessed=2**23, transcendentals=0),
        name=name,
    )(chosen, base, *ins)


def put_mixed(sizes, tokens, chosen, rows_in, branches, scales):
    def rows_of(tp, in_ref, scales_ref, *branch_refs):
        branch = branch_refs[0][:, branch_refs[0].shape[1] - in_ref.shape[1] :].astype(F32)
        for ref in branch_refs[1:]:
            branch += ref[...].astype(F32)
        return in_ref[...].astype(F32) + scales_ref[:, 0:1] * branch

    return put_rows(sizes, tokens, chosen, (rows_in, scales, *branches), rows_of, "put_mixed")


def put_grad(sizes, cotangent, chosen, rows_in, rows_grad, shares, scales, router):
    width = cotangent.shape[1]

    def rows_of(tp, in_ref, grad_ref, scales_ref, router_ref, *share_refs):
        gating, inverse_rows = scales_ref[:, 0:1], scales_ref[:, 1:2]
        wide_in = in_ref[...].astype(F32)
        summed = share_refs[0][...].astype(F32)
        for ref in share_refs[1:]:
            summed += ref[...].astype(F32)
        hidden, extra = summed[:, :width], summed[:, width:]
        row_stat = extra[:, 0:1] + extra[:, 2:3]
        logit_grad = (extra[:, 1:2] + extra[:, 3:4]) * (1.0 - gating)
        router_own = router_ref[:, pl.ds(pl.multiple_of(tp * width, width), width)].astype(F32)
        delta = inverse_rows * hidden - wide_in * (inverse_rows**3 * row_stat)
        delta = delta + logit_grad * router_own
        return grad_ref[...].astype(F32) + delta

    ins = (rows_in, rows_grad, scales, router, *shares)
    return put_rows(sizes, cotangent, chosen, ins, rows_of, "put_grad")


class Tiles:
    def __init__(self, picked, planes, columns, cores, heads):
        self.picked, self.planes, self.columns, self.cores, self.heads = (
            picked, planes, columns, cores, heads,
        )
        self.group = cores * picked
        self.lanes = heads * self.group
        self.keys = planes * picked
        self.half = heads * HEAD_DIM

    def fill(self, place, own, other, group_ref):
        core = place[2]
        mine = pl.ds(pl.multiple_of(core * self.picked, self.picked), self.picked)
        theirs = pl.ds(pl.multiple_of((1 - core) * self.picked, self.picked), self.picked)
        for s in range(self.columns):
            group_ref[s, mine, :] = own[s][...]
            group_ref[s, theirs, :] = other[s][...]

    def stacked(self, group_ref, s, first):
        parts = [
            group_ref[s, :, first + h * HEAD_DIM : first + (h + 1) * HEAD_DIM]
            for h in range(self.heads)
        ]
        return jnp.concatenate(parts, axis=0)

    def y_of(self, place, s):
        return lax.rem(place[1] + self.columns - s, self.columns)

    def scores(self, place, keys, queries, s):
        z, y, core = place[0], place[1], place[2]
        plane_rows = self.columns * self.group
        logits = mm(keys, queries, NT) * (LOG2E / math.sqrt(HEAD_DIM))
        key = lax.broadcasted_iota(jnp.int32, (self.keys, 1), 0)
        key_rank = (
            lax.div(key, self.picked) * plane_rows
            + (y * self.cores + core) * self.picked
            + lax.rem(key, self.picked)
        )
        lane = lax.broadcasted_iota(jnp.int32, (1, self.lanes), 1)
        query_rank = z * plane_rows + self.y_of(place, s) * self.group + lax.rem(lane, self.group)
        return jnp.where(key_rank <= query_rank, logits, FLOOR)


def softmax_parts(tiles, own, other, key_values):
    n = tiles.columns

    def kernel(kv_ref, *refs):
        own_refs, other_refs, out_ref, group_ref = refs[:n], refs[n : 2 * n], refs[2 * n], refs[-1]
        at = my_place()
        tiles.fill(at, own_refs, other_refs, group_ref)
        keys, values = kv_ref[:, :HEAD_DIM], kv_ref[:, HEAD_DIM:]
        for s in range(n):
            queries = tiles.stacked(group_ref, s, 0)
            grads = tiles.stacked(group_ref, s, tiles.half)
            logits = tiles.scores(at, keys, queries, s)
            top = jnp.max(logits, axis=0, keepdims=True)
            weights = jnp.exp2(logits - top)
            prob_grad = mm(values, grads, NT)
            total = jnp.sum(weights, axis=0, keepdims=True)
            inner = jnp.sum(weights * prob_grad, axis=0, keepdims=True)
            some = top > 0.5 * FLOOR
            slot = tiles.y_of(at, s)
            out_ref[slot, 0:1, :] = jnp.where(some, top + jnp.log(total) * LOG2E, FLOOR)
            out_ref[slot, 1:2, :] = jnp.where(some, inner / total, 0.0)

    return pl.pallas_call(
        kernel,
        in_specs=[whole()] * (1 + 2 * n),
        out_specs=whole(),
        out_shape=jax.ShapeDtypeStruct((n, 2, tiles.lanes), F32),
        scratch_shapes=[pltpu.VMEM((n, tiles.group, 2 * tiles.half), BF)],
        compiler_params=params(24),
        name="softmax_parts",
    )(key_values, *own, *other)


def attention_parts(tiles, own, other, key_values, parts):
    n = tiles.columns
    scale = 1.0 / math.sqrt(HEAD_DIM)

    def kernel(kv_ref, parts_ref, *refs):
        own_refs, other_refs = refs[:n], refs[n : 2 * n]
        mine_ref, theirs_ref, kv_grad_ref, group_ref, result_ref = refs[2 * n :]
        at = my_place()
        tiles.fill(at, own_refs, other_refs, group_ref)
        keys, values = kv_ref[:, :HEAD_DIM], kv_ref[:, HEAD_DIM:]
        keys_t, values_t = keys.T, values.T
        key_grad = jnp.zeros((tiles.keys, HEAD_DIM), F32)
        value_grad = jnp.zeros((tiles.keys, HEAD_DIM), F32)
        core = at[2]
        mine = pl.ds(pl.multiple_of(core * tiles.picked, tiles.picked), tiles.picked)
        theirs = pl.ds(pl.multiple_of((1 - core) * tiles.picked, tiles.picked), tiles.picked)
        for s in range(n):
            slot = tiles.y_of(at, s)
            tops = [parts_ref[b, slot, 0:1, :] for b in range(n * tiles.cores)]
            top = tops[0]
            for one in tops[1:]:
                top = jnp.maximum(top, one)
            total, inner = jnp.zeros_like(top), jnp.zeros_like(top)
            for b in range(n * tiles.cores):
                weight = jnp.exp2(tops[b] - top)
                total += weight
                inner += weight * parts_ref[b, slot, 1:2, :]
            shift = top + jnp.log(total) * LOG2E
            row_inner = inner / total
            queries = tiles.stacked(group_ref, s, 0)
            grads = tiles.stacked(group_ref, s, tiles.half)
            probs = jnp.exp2(tiles.scores(at, keys, queries, s) - shift)
            prob_grad = mm(values, grads, NT)
            score_low = (probs * (prob_grad - row_inner)).astype(BF)
            probs_low = probs.astype(BF)
            key_grad += mm(score_low, queries, NN)
            value_grad += mm(probs_low, grads, NN)
            query_t = mm(keys_t, score_low, NN) * scale
            output_t = mm(values_t, probs_low, NN)
            for h in range(tiles.heads):
                lanes = slice(h * tiles.group, (h + 1) * tiles.group)
                columns = slice(h * HEAD_DIM, (h + 1) * HEAD_DIM)
                shifted = slice(tiles.half + h * HEAD_DIM, tiles.half + (h + 1) * HEAD_DIM)
                result_ref[s, :, columns] = query_t[:, lanes].T.astype(BF)
                result_ref[s, :, shifted] = output_t[:, lanes].T.astype(BF)
            mine_ref[s, :, :] = result_ref[s, mine, :]
            theirs_ref[s, :, :] = result_ref[s, theirs, :]
        kv_grad_ref[:, :HEAD_DIM] = (key_grad * scale).astype(BF)
        kv_grad_ref[:, HEAD_DIM:] = value_grad.astype(BF)

    rows = like((n, tiles.picked, 2 * tiles.half))
    outs = [rows, rows, like((tiles.keys, 2 * HEAD_DIM))]
    return pl.pallas_call(
        kernel,
        in_specs=[whole()] * (2 + 2 * n),
        out_specs=[whole()] * 3,
        out_shape=outs,
        scratch_shapes=[pltpu.VMEM((n, tiles.group, 2 * tiles.half), BF)] * 2,
        compiler_params=params(24),
        name="attention_parts",
    )(key_values, parts, *own, *other)


def copies(array, count):
    return jnp.broadcast_to(array[None], (count,) + array.shape)


def exchange(array, axis):
    return lax.all_to_all(array, axis, 0, 0, tiled=True)


def shifted(array, axis, count, step):
    return lax.ppermute(array, axis, [(i, (i + step) % count) for i in range(count)])


def around_ring(piece, axis, count):
    pieces = [piece, shifted(piece, axis, count, 1)]
    if count == 2:
        return pieces
    last = shifted(piece, axis, count, count - 1)
    return pieces + [shifted(last, axis, count, count - 1), last]


def around_tp(shares, count):
    return [shares[0]] + [shifted(shares[s], "tp", count, s) for s in range(1, count)]


def on_device(sizes, tokens, chosen, router, w_query, w_key, w_value, w_out, cotangent):
    planes, columns, cores, parts_tp = sizes
    picked = chosen.shape[0]
    chosen, router = chosen[None, :], router[None, :]
    tiles = Tiles(picked, planes, columns, cores, w_query.shape[1] // HEAD_DIM)

    rows_grad = pick_rows(sizes, cotangent, chosen)
    grads = around_ring(rows_grad, "tp", parts_tp)
    rows_in = pick_rows(sizes, tokens, chosen)
    inputs = [rows_in] + [shifted(rows_in, "tp", parts_tp, s) for s in range(1, parts_tp)]
    near = touch((w_out, w_key, w_value), rows_in)
    key_values, mine, scales = project(
        sizes, inputs, grads, router, w_query, w_key, w_value, w_out, near
    )
    own = [mine] + [shifted(mine, "y", columns, s) for s in range(1, columns)]
    key_values = exchange(key_values, "z").reshape(tiles.keys, 2 * HEAD_DIM)
    key_values, *own = lax.optimization_barrier((key_values, *own))
    other = [shifted(piece, "core", cores, 1) for piece in own]
    parts = softmax_parts(tiles, own, other, key_values)
    parts = exchange(copies(parts, columns * cores), ("y", "core"))
    mine, theirs, kv_grads = attention_parts(tiles, own, other, key_values, parts)

    kv_grads = exchange(kv_grads.reshape(planes, picked, 2 * HEAD_DIM), "z")
    chip = add_pieces(mine, shifted(theirs, "core", cores, 1))
    pieces = [chip[0]] + [shifted(chip[s], "y", columns, columns - s) for s in range(1, columns)]
    near = touch((w_out,), chip[0])
    branches = branch_share(pieces, w_out, parts_tp, near)
    shares = hidden_share(branches[0], kv_grads, inputs, own[0], w_query, w_key, w_value)
    branches = around_tp(branches, parts_tp)
    shares = around_tp(shares, parts_tp)
    mixed = put_mixed(sizes, tokens, chosen, rows_in, branches, scales)
    input_grad = put_grad(
        sizes, cotangent, chosen, rows_in, rows_grad, shares, scales, router
    )
    return mixed, input_grad


def solution(mesh):
    sizes = (8, 4, 2, 4)
    return build(mesh, sizes)


def build(mesh, sizes):
    fine = Mesh(mesh.devices.reshape(sizes), ("z", "y", "core", "tp"))
    ctx = ("z", "y", "core")

    def step(*arrays):
        return on_device(sizes, *arrays)

    placed = (
        P(ctx, "tp"), P(ctx), P(), P(None, "tp"), P(None, "tp"), P(None, "tp"), P("tp", None), P(ctx, "tp"),
    )
    return jax.shard_map(
        step,
        mesh=fine,
        in_specs=placed,
        out_specs=(P(ctx, "tp"), P(ctx, "tp")),
        check_vma=False,
    )
```
